512 devices in a mesh: slab: 32 (over z, x_hi), iface: 4 (over y), mech: 4 (over x_lo, core).
Axes of the slice: x: 4 (x_hi: 2, x_lo: 2; x = x_hi * 2 + x_lo), y: 4, z: 16, core: 2. Of those that a mesh axis runs over, the one named last changes fastest.
Arguments:
- temp_start: float32 [256, 4, 128, 512], P(('slab', 'mech'), 'iface'), may hold values from 0.5 to 3
- conductivity: float32 [256, 4, 128, 512], P(('slab', 'mech'), 'iface'), may hold values from 0.3 to 2.8
- gap_conductance: float32 [256, 4, 128], P(('slab', 'mech'), 'iface'), may hold values from 10 to 20
- partner: int32 [512], P('iface'), may hold values from 0 to 511, each once
- row_order: int32 [4, 128], P('iface'), may hold values from 0 to 127, each once within a row
- active_layers: int32 [4, 128], P('iface', ('slab', 'mech')), may hold values from 1 to 32, as said below
- trial_stress: float32 [256, 4, 128, 512], P(None, 'iface', ('slab', 'mech')), may hold values from 0.5 to 2
Outputs:
- stress: float32 [256, 4, 128, 512], P(None, 'iface', ('slab', 'mech'))
- element_strain: float32 [32, 4, 128, 512], P(None, 'iface', ('slab', 'mech'))
The draws below stay inside these ranges and needn't reach their ends.
Inputs may be any that keep to these rules, and one draw needn't show every extreme that they name: `active_layers`: element layers that creep in one element row; some row has all 32.
All inputs are finite; a program needn't handle non-finite values.
Results may differ from the reference program's by a relative error of at most 0.00005.
Values sent between devices are 32-bit elements; how exact they have to be, the bound alone decides.
A program may use at most 64 MiB of HBM per device.

```python
import math
import jax
import jax.numpy as jnp

NR = 512
SWEEPS = 2
NEWTON = 4
SECTIONS = 4
CA = 128
NA = 512
NZ = 256


def draw_temp_start(key, part):
    first, second = jax.random.split(key)
    shape = (NZ, SECTIONS, CA, NR)
    coin = jax.random.uniform(first, shape, jnp.float32)
    jitter = jax.random.uniform(second, shape, jnp.float32)
    hot = coin < 0.5
    spread = 0.1 * jitter
    return jnp.where(hot, 3.0 - spread, 0.5 + spread).astype(jnp.float32)


def draw_conductivity(key, part):
    shape = (NZ, SECTIONS, CA, NR)
    unit = jax.random.uniform(key, shape, jnp.float32)
    radial = jnp.arange(NR, dtype=jnp.int32)
    middle = NR // 2
    near_face = ((radial >= middle - 2) & (radial <= middle + 1))[None, None, None, :]
    wide = 0.3 * jnp.exp(unit * math.log(2.8 / 0.3))
    close = 1.5 * jnp.exp(unit * math.log(2.0 / 1.5))
    return jnp.where(near_face, close, wide).astype(jnp.float32)


def draw_active_layers(key, part):
    first, second, third = jax.random.split(key, 3)
    top = NZ // 8
    draw_one = jax.random.randint(first, (SECTIONS, CA), 1, top + 1)
    draw_two = jax.random.randint(second, (SECTIONS, CA), 1, top + 1)
    upper = jnp.maximum(draw_one, draw_two).reshape(-1)
    chosen = jax.random.randint(third, (), 0, SECTIONS * CA)
    upper = jnp.where(jnp.arange(SECTIONS * CA) == chosen, top, upper)
    return upper.reshape(SECTIONS, CA).astype(jnp.int32)


def block_levels(rng, extent, cuts, least, largest):
    loudness = 1.0
    for axis_at, parts in cuts:
        heights = jax.random.uniform(jax.random.fold_in(jax.random.fold_in(rng, 6), axis_at), (parts,), jnp.float32, least / len(cuts), largest / len(cuts))
        loudness = loudness * jnp.repeat(jnp.exp(heights), extent[axis_at] // parts).reshape((-1,) + (1,) * (len(extent) - 1 - axis_at))
    return loudness


def setup_inputs(seed: int = 0) -> dict:
    keys = jax.random.split(jax.random.key(seed), 8)
    return {
        "temp_start": draw_temp_start(jax.random.fold_in(keys[7], 71), 0),
        "conductivity": draw_conductivity(jax.random.fold_in(keys[7], 71), 0),
        "gap_conductance": jnp.clip(jnp.exp(math.log(20.0) - 0.6931472 * jax.random.uniform(keys[2], (NZ, SECTIONS, CA), jnp.float32) ** block_levels(keys[2], (NZ, SECTIONS, CA), ((0, 128), (1, 4)), -0.2, 0.2)), 10.0, 20.0),
        "partner": jax.random.permutation(keys[3], NA).astype(jnp.int32),
        "row_order": jax.vmap(lambda own: jax.random.permutation(own, CA))(jax.random.split(keys[4], SECTIONS)).reshape((SECTIONS, CA)).astype(jnp.int32),
        "active_layers": draw_active_layers(jax.random.fold_in(keys[7], 71), 0),
        "trial_stress": jnp.clip(jnp.exp(math.log(2.0) - 1.3862944 * jax.random.uniform(keys[6], (NZ, SECTIONS, CA, NR), jnp.float32) ** block_levels(keys[6], (NZ, SECTIONS, CA, NR), ((1, 4), (2, 128)), -0.2, 0.2)), 0.5, 2.0),
    }


FLUX_STEP = 0.03
CREEP_RATE = 200.0
ACTIVATION = 12.0
REFERENCE_TEMP = 1.0


def neighbour_weight(shift_z, shift_a, shift_r):
    reach = abs(shift_z) + abs(shift_a) + abs(shift_r)
    return [0.0, 1.0, 0.5, 0.25][reach]


def conduction(padded_temp, padded_cond):
    center_temp = padded_temp[1:-1, 1:-1, 1:-1]
    center_cond = padded_cond[1:-1, 1:-1, 1:-1]
    depth, across, radial = center_temp.shape
    radial_index = jnp.arange(radial, dtype=jnp.int32)
    gap_row = radial // 2
    outward_open = (radial_index != gap_row - 1).astype(jnp.float32)
    inward_open = (radial_index != gap_row).astype(jnp.float32)
    total = jnp.zeros(center_temp.shape, jnp.float32)
    for shift_z in (-1, 0, 1):
        for shift_a in (-1, 0, 1):
            for shift_r in (-1, 0, 1):
                if shift_z == 0 and shift_a == 0 and shift_r == 0:
                    continue
                near_temp = padded_temp[1 + shift_z:1 + shift_z + depth, 1 + shift_a:1 + shift_a + across, 1 + shift_r:1 + shift_r + radial]
                near_cond = padded_cond[1 + shift_z:1 + shift_z + depth, 1 + shift_a:1 + shift_a + across, 1 + shift_r:1 + shift_r + radial]
                face = neighbour_weight(shift_z, shift_a, shift_r) * 0.5 * (center_cond + near_cond)
                if shift_r == 1:
                    face = face * outward_open
                elif shift_r == -1:
                    face = face * inward_open
                total = total + face * (near_temp - center_temp)
    return FLUX_STEP * total


def creep_return(mech_temp, trial, active_layers):
    rate = CREEP_RATE * jnp.exp(-ACTIVATION / (mech_temp + REFERENCE_TEMP))
    slip = jnp.zeros(trial.shape, jnp.float32)
    for newton_step in range(NEWTON):
        left = trial - slip
        residue = slip - rate * left ** 3
        slope = 1.0 + 3.0 * rate * left ** 2
        slip = slip - residue / slope
    depth = trial.shape[0]
    layer = jnp.arange(depth, dtype=jnp.int32) // 8
    live = (layer[:, None, None] < active_layers[None, :, :]).astype(jnp.float32)[..., None]
    creep = live * slip
    stress = trial - creep
    strain = jnp.sum(creep.reshape((depth // 8, 8) + trial.shape[1:]), axis=1) * 0.125
    return stress, strain


def reference(temp_start, conductivity, gap_conductance, partner, row_order, active_layers, trial_stress):
    depth, sections, rows, radial = temp_start.shape
    temp = temp_start.reshape(depth, sections * rows, radial)
    cond = conductivity.reshape(depth, sections * rows, radial)
    gap = gap_conductance.reshape(depth, sections * rows)
    padded_cond = jnp.pad(cond, 1)
    gap_row = radial // 2
    for sweep in range(SWEEPS):
        compact = temp[:, :, gap_row - 1]
        canister = temp[:, :, gap_row]
        flux = gap * (compact[:, partner] - canister)
        returned = jnp.zeros(flux.shape, jnp.float32).at[:, partner].add(flux)
        fresh = temp + conduction(jnp.pad(temp, 1), padded_cond)
        temp = fresh.at[:, :, gap_row].add(FLUX_STEP * flux).at[:, :, gap_row - 1].add(-FLUX_STEP * returned)
    grouped = temp.reshape(depth, sections, rows, radial)
    order = jnp.broadcast_to(row_order[None, :, :, None], grouped.shape).astype(jnp.int32)
    mech_temp = jnp.take_along_axis(grouped, order, axis=2)
    return creep_return(mech_temp, trial_stress, active_layers)
```

```python
import functools

import jax
import jax.numpy as jnp
from jax import lax
from jax.experimental import pallas as pl
from jax.experimental.pallas import tpu as pltpu
from jax.sharding import PartitionSpec as P

MESH = pl.DeviceIdType.MESH
NEWTON = 4
STEP = 0.03
CREEP_RATE = 200.0
ACTIVATION = 12.0
REFERENCE_TEMP = 1.0
LANES = 128
PAD = 8
CHUNK = 32


def kernel(
    slabs,
    sections,
    mechs,
    temp_ref,
    cond_ref,
    gap_ref,
    partner_ref,
    order_ref,
    active_ref,
    trial_ref,
    stress_ref,
    strain_ref,
    own_t,
    own_k,
    halo,
    fresh,
    halo2,
    u,
    keep,
    addend,
    cols,
    xbuf,
    hot,
    edge_out,
    edge_in,
    corner_in,
    edge_out2,
    edge_in2,
    corner_in2,
    packed,
    send,
    recv,
    trial_v,
    stress_v,
    strain_v,
    load_sem,
    out_sem,
    send_sem,
    layer_sem,
    edge_sem,
    corner_sem,
    layer2_sem,
    edge2_sem,
    corner2_sem,
    spread_send_sem,
    spread_sem,
    ready_sem,
):
    n = slabs * mechs
    group = 2 * mechs
    groups = n // group
    rows = own_t.shape[1]
    me = lax.axis_index("slab") * mechs + lax.axis_index("mech")
    y = lax.axis_index("iface")
    mine, place = me // group, me % group
    below, above = (me + n - 1) % n, (me + 1) % n
    y_low, y_high, y_far = (y + sections - 1) % sections, (y + 1) % sections, (y + 2) % sections

    def device(k, section):
        return (k // mechs, section, k % mechs)

    load_t = pltpu.make_async_copy(temp_ref, own_t, load_sem.at[0])
    load_k = pltpu.make_async_copy(cond_ref, own_k, load_sem.at[1])
    load_trial = pltpu.make_async_copy(trial_ref, trial_v, load_sem.at[2])
    load_t.start()
    load_k.start()

    barrier = pltpu.get_barrier_semaphore()

    def greet(k, section):
        pl.semaphore_signal(barrier, inc=1, device_id=device(k, section), device_id_type=MESH)

    near = [
        (below, y), (above, y), (me, y_low), (me, y_high), (me, y_far),
        (below, y_low), (below, y_high), (above, y_low), (above, y_high),
    ]
    for k, section in near:
        greet(k, section)
    for step in range(1, group):
        greet(mine * group + (place + step) % group, y)
    for step in range(1, groups):
        greet(((mine + step) % groups) * group + place, y)

    load_trial.start()
    row_of = lax.broadcasted_iota(jnp.int32, (rows, LANES), 0)
    lane_of = lax.broadcasted_iota(jnp.int32, (rows, LANES), 1)
    diagonal = row_of == lane_of

    def as_row(column):
        return jnp.sum(jnp.where(diagonal, column, 0.0), axis=0, keepdims=True)

    def as_column(row):
        return jnp.sum(jnp.where(diagonal, row, 0.0), axis=1, keepdims=True)

    base = (y * rows).astype(jnp.float32)
    whole = float(sections * rows)

    def relative(index):
        shifted = index - base
        return jnp.where(shifted < 0.0, shifted + whole, shifted)

    partner_row = partner_ref[...].astype(jnp.float32)
    partner_column = as_column(relative(partner_row))
    cols[:, 0:1] = as_column(gap_ref[0:1, :])
    cols[:, 1:2] = as_column(gap_ref[1:2, :])
    for q in range(sections):
        at = lax.broadcasted_iota(jnp.int32, (rows, LANES), 1).astype(jnp.float32) + float(q * rows)
        hot[0:rows, q * LANES : (q + 1) * LANES] = jnp.where(at == partner_column, 1.0, 0.0).astype(jnp.bfloat16)
    load_t.wait()
    load_k.wait()
    zeros_row = jnp.zeros((1, LANES), jnp.float32)
    for e, at in ((0, 0), (1, rows - 1)):
        for layer in range(2):
            edge_out[e, layer : layer + 1, :] = own_t[layer, at : at + 1, :]
            edge_out[e, 2 + layer : 3 + layer, :] = own_k[layer, at : at + 1, :]
    for layer in range(2):
        compact = as_row(own_t[layer, :, 2 * LANES - 1 : 2 * LANES])
        canister = as_row(own_t[layer, :, 2 * LANES : 2 * LANES + 1])
        for e in range(2):
            edge_out[e, 4:5, layer * LANES : (layer + 1) * LANES] = compact
            edge_out[e, 4:5, (2 + layer) * LANES : (3 + layer) * LANES] = canister
            edge_out[e, 5:6, layer * LANES : (layer + 1) * LANES] = gap_ref[layer : layer + 1, :]
    for e in range(2):
        edge_out[e, 5:6, 2 * LANES : 3 * LANES] = partner_row
        edge_out[e, 5:6, 3 * LANES : 4 * LANES] = zeros_row
        edge_out[e, 6:8, :] = jnp.zeros((2, 4 * LANES), jnp.float32)
        edge_out2[e] = jnp.zeros((8, 4 * LANES), jnp.float32)
    pl.semaphore_wait(barrier, len(near) + group - 1 + groups - 1)

    for step in range(1, groups):
        pl.semaphore_signal(
            ready_sem, inc=1, device_id=device(((mine + step) % groups) * group + place, y), device_id_type=MESH
        )

    def remote(source, target, sent, landed, k, section):
        return pltpu.make_async_remote_copy(
            src_ref=source, dst_ref=target, send_sem=sent, recv_sem=landed,
            device_id=device(k, section), device_id_type=MESH,
        )

    def edge_copies(out, into, corners, edge_landed, corner_landed, first):
        return [
            remote(out.at[1], into.at[0], send_sem.at[first], edge_landed.at[0], me, y_high),
            remote(out.at[0], into.at[1], send_sem.at[first + 1], edge_landed.at[1], me, y_low),
            remote(out.at[0], into.at[2], send_sem.at[first + 2], edge_landed.at[2], me, y_far),
            remote(out.at[1], corners.at[0, 0], send_sem.at[first + 3], corner_landed.at[0], above, y_high),
            remote(out.at[0], corners.at[0, 1], send_sem.at[first + 4], corner_landed.at[1], above, y_low),
            remote(out.at[1], corners.at[1, 0], send_sem.at[first + 5], corner_landed.at[2], below, y_high),
            remote(out.at[0], corners.at[1, 1], send_sem.at[first + 6], corner_landed.at[3], below, y_low),
        ]

    edges = edge_copies(edge_out, edge_in, corner_in, edge_sem, corner_sem, 0)
    for copy in edges:
        copy.start()
    layers = [
        remote(temp_ref.at[0], halo.at[1, 0], send_sem.at[7], layer_sem.at[1, 0], below, y),
        remote(temp_ref.at[1], halo.at[0, 0], send_sem.at[8], layer_sem.at[0, 0], above, y),
        remote(cond_ref.at[0], halo.at[1, 1], send_sem.at[9], layer_sem.at[1, 1], below, y),
        remote(cond_ref.at[1], halo.at[0, 1], send_sem.at[10], layer_sem.at[0, 1], above, y),
    ]
    for copy in layers:
        copy.start()

    has_below = jnp.where(me > 0, 0.5, 0.0).astype(jnp.float32)
    has_above = jnp.where(me < n - 1, 0.5, 0.0).astype(jnp.float32)
    has_low = jnp.where(y > 0, 1.0, 0.0).astype(jnp.float32)
    has_high = jnp.where(y < sections - 1, 1.0, 0.0).astype(jnp.float32)

    def across_layers(before, first, second, after):
        return (
            first + 0.5 * second + has_below * before,
            second + 0.5 * first + has_above * after,
        )

    def fill_edges(t_of, k_of, with_cond):
        for e, row, there in ((0, PAD - 1, has_low), (1, PAD + rows, has_high)):
            ts, ks = t_of(e), k_of(e)
            sums = [across_layers(*ts), across_layers(*[a * b for a, b in zip(ts, ks)])]
            if with_cond:
                sums.append(across_layers(*ks))
            for f, pair in enumerate(sums):
                for layer in range(2):
                    edge = there * pair[layer]
                    for c in range(4):
                        u[layer, f, c, row : row + 1, :] = edge[:, c * LANES : (c + 1) * LANES]

    def fill_rows(t_of, k_of, with_cond):
        def body(i, carry):
            start = pl.multiple_of(i * CHUNK, CHUNK)
            at = pl.ds(start, CHUNK)
            to = pl.ds(pl.multiple_of(start + PAD, 8), CHUNK)
            for c in range(4):
                ts, ks = t_of(at, c), k_of(at, c)
                sums = [across_layers(*ts), across_layers(*[a * b for a, b in zip(ts, ks)])]
                if with_cond:
                    sums.append(across_layers(*ks))
                for f, pair in enumerate(sums):
                    for layer in range(2):
                        u[layer, f, c, to, :] = pair[layer]
            return carry

        lax.fori_loop(0, rows // CHUNK, body, 0)

    lane = lax.broadcasted_iota(jnp.int32, (CHUNK, LANES), 1)
    first_lane, last_lane = lane == 0, lane == LANES - 1

    def spread_of(layer, f, c0, start):
        v = []
        for c in (c0, c0 + 1):
            mid = u[layer, f, c, pl.ds(start + PAD, CHUNK), :]
            up = u[layer, f, c, pl.ds(start + PAD - 1, CHUNK), :]
            down = u[layer, f, c, pl.ds(start + PAD + 1, CHUNK), :]
            v.append(mid + 0.5 * (up + down))
        right = [pltpu.roll(x, 1, 1) for x in v]
        left = [pltpu.roll(x, LANES - 1, 1) for x in v]
        return [
            v[0] + 0.5 * (jnp.where(first_lane, 0.0, right[0]) + jnp.where(last_lane, left[1], left[0])),
            v[1] + 0.5 * (jnp.where(first_lane, right[0], right[1]) + jnp.where(last_lane, 0.0, left[1])),
        ]

    def sweep(t_of, put, first):
        for layer in range(2):
            for half in range(2):
                for i in range(rows // CHUNK):
                    start = i * CHUNK
                    at = pl.ds(start, CHUNK)
                    spread_t = spread_of(layer, 0, 2 * half, start)
                    spread_kt = spread_of(layer, 1, 2 * half, start)
                    spread_k = spread_of(layer, 2, 2 * half, start) if first else None
                    for j in range(2):
                        c = 2 * half + j
                        k = own_k[layer, at, c * LANES : (c + 1) * LANES]
                        t = t_of(layer, at, c)
                        if first:
                            weight = jnp.full((CHUNK, LANES), 8.0, jnp.float32)
                            if c == 1:
                                weight = jnp.where(last_lane, 6.0, weight)
                            if c == 2:
                                weight = jnp.where(first_lane, 6.0, weight)
                            drain = weight * k + spread_k[j]
                            keep[layer, c, at, :] = drain
                        else:
                            drain = keep[layer, c, at, :]
                        new = t + STEP * (k * spread_t[j] + spread_kt[j] - t * drain)
                        if c in (1, 2):
                            new = new + addend[layer, c - 1, at, :]
                        put(layer, c, start, new)

    def gather(faces, into, slots):
        for q, block in enumerate([faces[0], *[into[s] for s in slots]]):
            for layer in range(4):
                xbuf[layer : layer + 1, q * LANES : (q + 1) * LANES] = block[4:5, layer * LANES : (layer + 1) * LANES]
            for layer in range(2):
                xbuf[4 + layer : 5 + layer, q * LANES : (q + 1) * LANES] = block[
                    5:6, layer * LANES : (layer + 1) * LANES
                ]
        x = xbuf[...]
        high = x.astype(jnp.bfloat16)
        rest = x - high.astype(jnp.float32)
        middle = rest.astype(jnp.bfloat16)
        low = (rest - middle.astype(jnp.float32)).astype(jnp.bfloat16)
        return sum(
            lax.dot_general(hot[...], part, (((1,), (1,)), ((), ())), preferred_element_type=jnp.float32)
            for part in (high, middle, low)
        )

    def gap_flux(found, face_of):
        for layer in range(2):
            compact, canister = face_of(layer)
            flux = cols[:, layer : layer + 1] * (found[0:rows, layer : layer + 1] - canister)
            returned = cols[:, 2 + layer : 3 + layer] * (compact - found[rows : 2 * rows, 2 + layer : 3 + layer])
            addend[layer, 0] = jnp.where(lane_of == LANES - 1, -STEP * returned, 0.0)
            addend[layer, 1] = jnp.where(lane_of == 0, STEP * flux, 0.0)

    xbuf[6:8, :] = jnp.zeros((2, 4 * LANES), jnp.float32)
    for copy in edges[:3]:
        copy.wait_recv()
    slots = (1, 2, 0)
    for q, block in enumerate([edge_out[0], *[edge_in[s] for s in slots]]):
        theirs = relative(block[5:6, 2 * LANES : 3 * LANES])
        hot[rows : 2 * rows, q * LANES : (q + 1) * LANES] = jnp.where(
            row_of.astype(jnp.float32) == theirs, 1.0, 0.0
        ).astype(jnp.bfloat16)
    found = gather(edge_out, edge_in, slots)
    cols[:, 2:4] = found[rows : 2 * rows, 4:6]
    gap_flux(
        found,
        lambda layer: (own_t[layer, :, 2 * LANES - 1 : 2 * LANES], own_t[layer, :, 2 * LANES : 2 * LANES + 1]),
    )
    for copy in edges[3:]:
        copy.wait_recv()

    def edge_layers(into, corners, row):
        def of(e):
            return (
                corners[0, e, row + 1 : row + 2, :],
                into[e, row : row + 1, :],
                into[e, row + 1 : row + 2, :],
                corners[1, e, row : row + 1, :],
            )

        return of

    fill_edges(edge_layers(edge_in, corner_in, 0), edge_layers(edge_in, corner_in, 2), True)
    for copy in layers:
        copy.wait_recv()

    def block(c):
        return slice(c * LANES, (c + 1) * LANES)

    def k_rows(at, c):
        return (halo[0, 1, at, block(c)], own_k[0, at, block(c)], own_k[1, at, block(c)], halo[1, 1, at, block(c)])

    fill_rows(
        lambda at, c: (halo[0, 0, at, block(c)], own_t[0, at, block(c)], own_t[1, at, block(c)], halo[1, 0, at, block(c)]),
        k_rows,
        True,
    )

    def put_fresh(layer, c, start, new):
        fresh[layer, c, pl.ds(start, CHUNK), :] = new

    sweep(lambda layer, at, c: own_t[layer, at, block(c)], put_fresh, True)

    layers2 = [
        remote(fresh.at[0], halo2.at[1], send_sem.at[18], layer2_sem.at[1], below, y),
        remote(fresh.at[1], halo2.at[0], send_sem.at[19], layer2_sem.at[0], above, y),
    ]
    for copy in layers2:
        copy.start()
    for e, at in ((0, 0), (1, rows - 1)):
        for layer in range(2):
            for c in range(4):
                edge_out2[e, layer : layer + 1, block(c)] = fresh[layer, c, at : at + 1, :]
    for layer in range(2):
        compact = as_row(fresh[layer, 1, :, LANES - 1 : LANES])
        canister = as_row(fresh[layer, 2, :, 0:1])
        for e in range(2):
            edge_out2[e, 4:5, layer * LANES : (layer + 1) * LANES] = compact
            edge_out2[e, 4:5, (2 + layer) * LANES : (3 + layer) * LANES] = canister
    edges2 = edge_copies(edge_out2, edge_in2, corner_in2, edge2_sem, corner2_sem, 11)
    for copy in edges2:
        copy.start()

    for copy in edges2[:3]:
        copy.wait_recv()
    found = gather(edge_out2, edge_in2, slots)
    gap_flux(found, lambda layer: (fresh[layer, 1, :, LANES - 1 : LANES], fresh[layer, 2, :, 0:1]))
    for copy in edges2[3:]:
        copy.wait_recv()
    fill_edges(edge_layers(edge_in2, corner_in2, 0), edge_layers(edge_in, corner_in, 2), False)
    for copy in layers2:
        copy.wait_recv()
    fill_rows(lambda at, c: (halo2[0, c, at, :], fresh[0, c, at, :], fresh[1, c, at, :], halo2[1, c, at, :]), k_rows, False)

    def put_packed(layer, c, start, new):
        packed[pl.ds(start, CHUNK), layer * 4 + c, :] = new

    sweep(lambda layer, at, c: fresh[layer, c, at, :], put_packed, False)

    pl.semaphore_wait(ready_sem, groups - 1)

    def pick(j):
        send[j] = packed[order_ref[0, j]]

    def target_group(i):
        return jnp.where(i % 2 == 1, groups // 2 - (i + 1) // 2, groups - groups // 2 + i // 2) % groups

    def spread(i, carry):
        other = (mine + target_group(i)) % groups
        for step in range(group):
            pick(other * group + step)
        for step in range(group):
            j = other * group + (place + step) % group
            remote(send.at[j], recv.at[me], spread_send_sem, spread_sem.at[mine], j, y).start()
        return carry

    lax.fori_loop(0, groups - 1, spread, 0)
    for step in range(group):
        pick(mine * group + step)
    for step in range(1, group):
        j = mine * group + (place + step) % group
        remote(send.at[j], recv.at[me], spread_send_sem, spread_sem.at[mine], j, y).start()
    pltpu.make_async_copy(send.at[me], recv.at[me], spread_sem.at[mine]).start()

    load_trial.wait()
    active = jnp.broadcast_to(active_ref[...], (8, LANES))
    upper = lax.broadcasted_iota(jnp.int32, (8, LANES), 0) < 4

    def creep(i, carry):
        g = (mine + groups - target_group(i)) % groups
        at = pl.ds(g * group, group)
        pltpu.make_async_copy(recv.at[at], recv.at[at], spread_sem.at[g]).wait()
        temp = recv[at]
        trial = trial_v[at]
        rate = CREEP_RATE * jnp.exp(-ACTIVATION / (temp + REFERENCE_TEMP))
        slip = jnp.zeros_like(trial)
        for newton in range(NEWTON):
            left = trial - slip
            pull = rate * (left * left)
            slip = slip - (slip - pull * left) / (1.0 + 3.0 * pull)
        sums = []
        for e in range(2):
            live = jnp.where(jnp.full((8, LANES), 2 * g + e, jnp.int32) < active, 1.0, 0.0)
            part = live * slip[4 * e : 4 * e + 4]
            stress_v[pl.ds(g * group + 4 * e, 4)] = trial[4 * e : 4 * e + 4] - part
            total = part[0] + part[1] + part[2] + part[3]
            sums.append((total + pltpu.roll(total, 4, 0)) * 0.125)
        strain_v[g] = jnp.where(upper, sums[0], sums[1])
        pltpu.make_async_copy(stress_v.at[at], stress_ref.at[at], out_sem.at[0]).start()
        return carry

    lax.fori_loop(0, groups, creep, 0)
    strain_copy = pltpu.make_async_copy(strain_v, strain_ref, out_sem.at[1])
    strain_copy.start()
    for copy in edges + layers + edges2 + layers2:
        copy.wait_send()
    most = pl.ds(0, n - 1)
    pltpu.make_async_copy(send.at[most], send.at[most], spread_send_sem).wait()
    pltpu.make_async_copy(stress_v, stress_ref, out_sem.at[0]).wait()
    strain_copy.wait()


def solution(mesh):
    slabs, sections, mechs = (mesh.shape[a] for a in ("slab", "iface", "mech"))
    n = slabs * mechs
    groups = n // (2 * mechs)

    def on_device(temp, cond, gap, partner, order, active, trial):
        depth, _, rows, radial = temp.shape
        f32 = jnp.float32
        any_space = pl.BlockSpec(memory_space=pl.ANY)
        vmem = pl.BlockSpec(memory_space=pltpu.VMEM)
        smem = pl.BlockSpec(memory_space=pltpu.SMEM)
        dma = pltpu.SemaphoreType.DMA
        stress, strain = pl.pallas_call(
            functools.partial(kernel, slabs, sections, mechs),
            out_shape=(
                jax.ShapeDtypeStruct((n, 8, LANES), f32),
                jax.ShapeDtypeStruct((groups, 8, LANES), f32),
            ),
            in_specs=[any_space, any_space, vmem, vmem, smem, vmem, any_space],
            out_specs=(any_space, any_space),
            scratch_shapes=[
                pltpu.VMEM((2, rows, radial), f32),
                pltpu.VMEM((2, rows, radial), f32),
                pltpu.VMEM((2, 2, rows, radial), f32),
                pltpu.VMEM((2, 4, rows, LANES), f32),
                pltpu.VMEM((2, 4, rows, LANES), f32),
                pltpu.VMEM((2, 3, 4, rows + 2 * PAD, LANES), f32),
                pltpu.VMEM((2, 4, rows, LANES), f32),
                pltpu.VMEM((2, 2, rows, LANES), f32),
                pltpu.VMEM((rows, LANES), f32),
                pltpu.VMEM((8, radial), f32),
                pltpu.VMEM((2 * rows, sections * rows), jnp.bfloat16),
                pltpu.VMEM((2, 8, radial), f32),
                pltpu.VMEM((3, 8, radial), f32),
                pltpu.VMEM((2, 2, 8, radial), f32),
                pltpu.VMEM((2, 8, radial), f32),
                pltpu.VMEM((3, 8, radial), f32),
                pltpu.VMEM((2, 2, 8, radial), f32),
                pltpu.VMEM((rows, 8, LANES), f32),
                pltpu.VMEM((n, 8, LANES), f32),
                pltpu.VMEM((n, 8, LANES), f32),
                pltpu.VMEM((n, 8, LANES), f32),
                pltpu.VMEM((n, 8, LANES), f32),
                pltpu.VMEM((groups, 8, LANES), f32),
                dma((3,)),
                dma((2,)),
                dma((20,)),
                dma((2, 2)),
                dma((3,)),
                dma((4,)),
                dma((2,)),
                dma((3,)),
                dma((4,)),
                dma,
                dma((groups,)),
                pltpu.SemaphoreType.REGULAR,
            ],
            compiler_params=pltpu.CompilerParams(
                collective_id=0, has_side_effects=True, vmem_limit_bytes=60 * 1024 * 1024
            ),
        )(
            temp.reshape(depth, rows, radial),
            cond.reshape(depth, rows, radial),
            gap.reshape(depth, rows),
            partner.reshape(1, rows),
            order,
            active,
            trial.reshape(n, 8, LANES),
        )
        return stress.reshape(trial.shape), strain.reshape(trial.shape[0] // 8, 1, 1, radial)

    placed = (
        P(("slab", "mech"), "iface", None, None),
        P(("slab", "mech"), "iface", None, None),
        P(("slab", "mech"), "iface", None),
        P("iface"),
        P("iface", None),
        P("iface", ("slab", "mech")),
        P(None, "iface", ("slab", "mech"), None),
    )
    return jax.shard_map(
        on_device,
        mesh=mesh,
        in_specs=placed,
        out_specs=(
            P(None, "iface", ("slab", "mech"), None),
            P(None, "iface", ("slab", "mech"), None),
        ),
        check_vma=False,
    )
```

```python
import functools

import jax
import jax.numpy as jnp
from jax import lax
from jax.experimental import pallas as pl
from jax.experimental.pallas import tpu as pltpu
from jax.sharding import PartitionSpec as P

MESH = pl.DeviceIdType.MESH
NEWTON = 4
STEP = 0.03
CREEP_RATE = 200.0
ACTIVATION = 12.0
REFERENCE_TEMP = 1.0
LANES = 128
PAD = 8
CHUNK = 32


def kernel(
    slabs,
    sections,
    mechs,
    temp_ref,
    cond_ref,
    gap_in,
    partner_in,
    order_in,
    active_in,
    trial_ref,
    stress_ref,
    strain_ref,
    gap_ref,
    partner_ref,
    order_ref,
    active_ref,
    own_t,
    own_k,
    halo,
    fresh,
    halo2,
    u,
    keep,
    addend,
    cols,
    xbuf,
    hot,
    edge_out,
    edge_in,
    corner_in,
    edge_out2,
    edge_in2,
    corner_in2,
    packed,
    send,
    recv,
    trial_v,
    load_sem,
    send_sem,
    layer_sem,
    edge_sem,
    corner_sem,
    layer2_sem,
    edge2_sem,
    corner2_sem,
    spread_send_sem,
    spread_sem,
    ready_sem,
):
    n = slabs * mechs
    group = 2 * mechs
    groups = n // group
    rows = own_t.shape[1]
    me = lax.axis_index("slab") * mechs + lax.axis_index("mech")
    y = lax.axis_index("iface")
    mine, place = me // group, me % group
    below, above = (me + n - 1) % n, (me + 1) % n
    y_low, y_high, y_far = (y + sections - 1) % sections, (y + 1) % sections, (y + 2) % sections

    def device(k, section):
        return (k // mechs, section, k % mechs)

    load_t = pltpu.make_async_copy(temp_ref, own_t, load_sem.at[0])
    load_k = pltpu.make_async_copy(cond_ref, own_k, load_sem.at[1])
    load_trial = pltpu.make_async_copy(trial_ref, trial_v, load_sem.at[2])
    load_gap = pltpu.make_async_copy(gap_in, gap_ref, load_sem.at[3])
    load_partner = pltpu.make_async_copy(partner_in, partner_ref, load_sem.at[4])
    load_order = pltpu.make_async_copy(order_in, order_ref, load_sem.at[5])
    load_active = pltpu.make_async_copy(active_in, active_ref, load_sem.at[6])
    for copy in (load_partner, load_gap, load_t, load_k, load_order, load_active):
        copy.start()

    barrier = pltpu.get_barrier_semaphore()

    def greet(k, section):
        pl.semaphore_signal(barrier, inc=1, device_id=device(k, section), device_id_type=MESH)

    near = [
        (below, y), (above, y), (me, y_low), (me, y_high), (me, y_far),
        (below, y_low), (below, y_high), (above, y_low), (above, y_high),
    ]
    for k, section in near:
        greet(k, section)
    for step in range(1, group):
        greet(mine * group + (place + step) % group, y)
    for step in (1, groups - 1):
        greet(((mine + step) % groups) * group + place, y)

    load_trial.start()
    row_of = lax.broadcasted_iota(jnp.int32, (rows, LANES), 0)
    lane_of = lax.broadcasted_iota(jnp.int32, (rows, LANES), 1)
    diagonal = row_of == lane_of

    def as_row(column):
        return jnp.sum(jnp.where(diagonal, column, 0.0), axis=0, keepdims=True)

    def as_column(row):
        return jnp.sum(jnp.where(diagonal, row, 0.0), axis=1, keepdims=True)

    base = (y * rows).astype(jnp.float32)
    whole = float(sections * rows)

    def relative(index):
        shifted = index - base
        return jnp.where(shifted < 0.0, shifted + whole, shifted)

    load_partner.wait()
    load_gap.wait()
    partner_row = partner_ref[...].astype(jnp.float32)
    partner_column = as_column(relative(partner_row))
    cols[:, 0:1] = as_column(gap_ref[0:1, :])
    cols[:, 1:2] = as_column(gap_ref[1:2, :])
    for q in range(sections):
        at = lax.broadcasted_iota(jnp.int32, (rows, LANES), 1).astype(jnp.float32) + float(q * rows)
        hot[0:rows, q * LANES : (q + 1) * LANES] = jnp.where(at == partner_column, 1.0, 0.0).astype(jnp.bfloat16)
    load_t.wait()
    load_k.wait()
    zeros_row = jnp.zeros((1, LANES), jnp.float32)
    for e, at in ((0, 0), (1, rows - 1)):
        for layer in range(2):
            edge_out[e, layer : layer + 1, :] = own_t[layer, at : at + 1, :]
            edge_out[e, 2 + layer : 3 + layer, :] = own_k[layer, at : at + 1, :]
    for layer in range(2):
        compact = as_row(own_t[layer, :, 2 * LANES - 1 : 2 * LANES])
        canister = as_row(own_t[layer, :, 2 * LANES : 2 * LANES + 1])
        for e in range(2):
            edge_out[e, 4:5, layer * LANES : (layer + 1) * LANES] = compact
            edge_out[e, 4:5, (2 + layer) * LANES : (3 + layer) * LANES] = canister
            edge_out[e, 5:6, layer * LANES : (layer + 1) * LANES] = gap_ref[layer : layer + 1, :]
    for e in range(2):
        edge_out[e, 5:6, 2 * LANES : 3 * LANES] = partner_row
        edge_out[e, 5:6, 3 * LANES : 4 * LANES] = zeros_row
        edge_out[e, 6:8, :] = jnp.zeros((2, 4 * LANES), jnp.float32)
        edge_out2[e] = jnp.zeros((8, 4 * LANES), jnp.float32)
    pl.semaphore_wait(barrier, len(near) + group - 1 + 2)

    def tell(level):
        for step in sorted({2**level, groups - 2**level}):
            other = ((mine + step) % groups) * group + place
            pl.semaphore_signal(ready_sem.at[level], inc=1, device_id=device(other, y), device_id_type=MESH)

    def hear(level):
        pl.semaphore_wait(ready_sem.at[level], len({2**level, groups - 2**level}))

    tell(0)

    def remote(source, target, sent, landed, k, section):
        return pltpu.make_async_remote_copy(
            src_ref=source, dst_ref=target, send_sem=sent, recv_sem=landed,
            device_id=device(k, section), device_id_type=MESH,
        )

    def edge_copies(out, into, corners, edge_landed, corner_landed, first):
        return [
            remote(out.at[1], into.at[0], send_sem.at[first], edge_landed.at[0], me, y_high),
            remote(out.at[0], into.at[1], send_sem.at[first + 1], edge_landed.at[1], me, y_low),
            remote(out.at[0], into.at[2], send_sem.at[first + 2], edge_landed.at[2], me, y_far),
            remote(out.at[1], corners.at[0, 0], send_sem.at[first + 3], corner_landed.at[0], above, y_high),
            remote(out.at[0], corners.at[0, 1], send_sem.at[first + 4], corner_landed.at[1], above, y_low),
            remote(out.at[1], corners.at[1, 0], send_sem.at[first + 5], corner_landed.at[2], below, y_high),
            remote(out.at[0], corners.at[1, 1], send_sem.at[first + 6], corner_landed.at[3], below, y_low),
        ]

    edges = edge_copies(edge_out, edge_in, corner_in, edge_sem, corner_sem, 0)
    for copy in edges:
        copy.start()
    layers = [
        remote(temp_ref.at[0], halo.at[1, 0], send_sem.at[7], layer_sem.at[1, 0], below, y),
        remote(temp_ref.at[1], halo.at[0, 0], send_sem.at[8], layer_sem.at[0, 0], above, y),
        remote(cond_ref.at[0], halo.at[1, 1], send_sem.at[9], layer_sem.at[1, 1], below, y),
        remote(cond_ref.at[1], halo.at[0, 1], send_sem.at[10], layer_sem.at[0, 1], above, y),
    ]
    for copy in layers:
        copy.start()

    has_below = jnp.where(me > 0, 0.5, 0.0).astype(jnp.float32)
    has_above = jnp.where(me < n - 1, 0.5, 0.0).astype(jnp.float32)
    has_low = jnp.where(y > 0, 1.0, 0.0).astype(jnp.float32)
    has_high = jnp.where(y < sections - 1, 1.0, 0.0).astype(jnp.float32)

    def across_layers(before, first, second, after):
        return (
            first + 0.5 * second + has_below * before,
            second + 0.5 * first + has_above * after,
        )

    def fill_edges(t_of, k_of, with_cond):
        for e, row, there in ((0, PAD - 1, has_low), (1, PAD + rows, has_high)):
            ts, ks = t_of(e), k_of(e)
            sums = [across_layers(*ts), across_layers(*[a * b for a, b in zip(ts, ks)])]
            if with_cond:
                sums.append(across_layers(*ks))
            for f, pair in enumerate(sums):
                for layer in range(2):
                    edge = there * pair[layer]
                    for c in range(4):
                        u[layer, f, c, row : row + 1, :] = edge[:, c * LANES : (c + 1) * LANES]

    def fill_rows(t_of, k_of, with_cond):
        def body(i, carry):
            start = pl.multiple_of(i * CHUNK, CHUNK)
            at = pl.ds(start, CHUNK)
            to = pl.ds(pl.multiple_of(start + PAD, 8), CHUNK)
            for c in range(4):
                ts, ks = t_of(at, c), k_of(at, c)
                sums = [across_layers(*ts), across_layers(*[a * b for a, b in zip(ts, ks)])]
                if with_cond:
                    sums.append(across_layers(*ks))
                for f, pair in enumerate(sums):
                    for layer in range(2):
                        u[layer, f, c, to, :] = pair[layer]
            return carry

        lax.fori_loop(0, rows // CHUNK, body, 0)

    lane = lax.broadcasted_iota(jnp.int32, (CHUNK, LANES), 1)
    first_lane, last_lane = lane == 0, lane == LANES - 1

    def spread_of(layer, f, c0, start):
        v = []
        for c in (c0, c0 + 1):
            mid = u[layer, f, c, pl.ds(start + PAD, CHUNK), :]
            up = u[layer, f, c, pl.ds(start + PAD - 1, CHUNK), :]
            down = u[layer, f, c, pl.ds(start + PAD + 1, CHUNK), :]
            v.append(mid + 0.5 * (up + down))
        right = [pltpu.roll(x, 1, 1) for x in v]
        left = [pltpu.roll(x, LANES - 1, 1) for x in v]
        return [
            v[0] + 0.5 * (jnp.where(first_lane, 0.0, right[0]) + jnp.where(last_lane, left[1], left[0])),
            v[1] + 0.5 * (jnp.where(first_lane, right[0], right[1]) + jnp.where(last_lane, 0.0, left[1])),
        ]

    def sweep(t_of, put, first):
        for layer in range(2):
            for half in range(2):
                for i in range(rows // CHUNK):
                    start = i * CHUNK
                    at = pl.ds(start, CHUNK)
                    spread_t = spread_of(layer, 0, 2 * half, start)
                    spread_kt = spread_of(layer, 1, 2 * half, start)
                    spread_k = spread_of(layer, 2, 2 * half, start) if first else None
                    for j in range(2):
                        c = 2 * half + j
                        k = own_k[layer, at, c * LANES : (c + 1) * LANES]
                        t = t_of(layer, at, c)
                        if first:
                            weight = jnp.full((CHUNK, LANES), 8.0, jnp.float32)
                            if c == 1:
                                weight = jnp.where(last_lane, 6.0, weight)
                            if c == 2:
                                weight = jnp.where(first_lane, 6.0, weight)
                            drain = weight * k + spread_k[j]
                            keep[layer, c, at, :] = drain
                        else:
                            drain = keep[layer, c, at, :]
                        new = t + STEP * (k * spread_t[j] + spread_kt[j] - t * drain)
                        if c in (1, 2):
                            new = new + addend[layer, c - 1, at, :]
                        put(layer, c, start, new)

    def gather(faces, into, slots):
        for q, block in enumerate([faces[0], *[into[s] for s in slots]]):
            for layer in range(4):
                xbuf[layer : layer + 1, q * LANES : (q + 1) * LANES] = block[4:5, layer * LANES : (layer + 1) * LANES]
            for layer in range(2):
                xbuf[4 + layer : 5 + layer, q * LANES : (q + 1) * LANES] = block[
                    5:6, layer * LANES : (layer + 1) * LANES
                ]
        x = xbuf[...]
        high = x.astype(jnp.bfloat16)
        rest = x - high.astype(jnp.float32)
        middle = rest.astype(jnp.bfloat16)
        low = (rest - middle.astype(jnp.float32)).astype(jnp.bfloat16)
        return sum(
            lax.dot_general(hot[...], part, (((1,), (1,)), ((), ())), preferred_element_type=jnp.float32)
            for part in (high, middle, low)
        )

    def gap_flux(found, face_of):
        for layer in range(2):
            compact, canister = face_of(layer)
            flux = cols[:, layer : layer + 1] * (found[0:rows, layer : layer + 1] - canister)
            returned = cols[:, 2 + layer : 3 + layer] * (compact - found[rows : 2 * rows, 2 + layer : 3 + layer])
            addend[layer, 0] = jnp.where(lane_of == LANES - 1, -STEP * returned, 0.0)
            addend[layer, 1] = jnp.where(lane_of == 0, STEP * flux, 0.0)

    hear(0)
    tell(1)
    xbuf[6:8, :] = jnp.zeros((2, 4 * LANES), jnp.float32)
    for copy in edges[:3]:
        copy.wait_recv()
    slots = (1, 2, 0)
    for q, block in enumerate([edge_out[0], *[edge_in[s] for s in slots]]):
        theirs = relative(block[5:6, 2 * LANES : 3 * LANES])
        hot[rows : 2 * rows, q * LANES : (q + 1) * LANES] = jnp.where(
            row_of.astype(jnp.float32) == theirs, 1.0, 0.0
        ).astype(jnp.bfloat16)
    found = gather(edge_out, edge_in, slots)
    cols[:, 2:4] = found[rows : 2 * rows, 4:6]
    gap_flux(
        found,
        lambda layer: (own_t[layer, :, 2 * LANES - 1 : 2 * LANES], own_t[layer, :, 2 * LANES : 2 * LANES + 1]),
    )
    for copy in edges[3:]:
        copy.wait_recv()

    def edge_layers(into, corners, row):
        def of(e):
            return (
                corners[0, e, row + 1 : row + 2, :],
                into[e, row : row + 1, :],
                into[e, row + 1 : row + 2, :],
                corners[1, e, row : row + 1, :],
            )

        return of

    fill_edges(edge_layers(edge_in, corner_in, 0), edge_layers(edge_in, corner_in, 2), True)
    hear(1)
    tell(2)
    for copy in layers:
        copy.wait_recv()

    def block(c):
        return slice(c * LANES, (c + 1) * LANES)

    def k_rows(at, c):
        return (halo[0, 1, at, block(c)], own_k[0, at, block(c)], own_k[1, at, block(c)], halo[1, 1, at, block(c)])

    fill_rows(
        lambda at, c: (halo[0, 0, at, block(c)], own_t[0, at, block(c)], own_t[1, at, block(c)], halo[1, 0, at, block(c)]),
        k_rows,
        True,
    )

    def put_fresh(layer, c, start, new):
        fresh[layer, c, pl.ds(start, CHUNK), :] = new

    sweep(lambda layer, at, c: own_t[layer, at, block(c)], put_fresh, True)

    layers2 = [
        remote(fresh.at[0], halo2.at[1], send_sem.at[18], layer2_sem.at[1], below, y),
        remote(fresh.at[1], halo2.at[0], send_sem.at[19], layer2_sem.at[0], above, y),
    ]
    for copy in layers2:
        copy.start()
    for e, at in ((0, 0), (1, rows - 1)):
        for layer in range(2):
            for c in range(4):
                edge_out2[e, layer : layer + 1, block(c)] = fresh[layer, c, at : at + 1, :]
    for layer in range(2):
        compact = as_row(fresh[layer, 1, :, LANES - 1 : LANES])
        canister = as_row(fresh[layer, 2, :, 0:1])
        for e in range(2):
            edge_out2[e, 4:5, layer * LANES : (layer + 1) * LANES] = compact
            edge_out2[e, 4:5, (2 + layer) * LANES : (3 + layer) * LANES] = canister
    edges2 = edge_copies(edge_out2, edge_in2, corner_in2, edge2_sem, corner2_sem, 11)
    for copy in edges2:
        copy.start()

    hear(2)
    tell(3)

    for copy in edges2[:3]:
        copy.wait_recv()
    found = gather(edge_out2, edge_in2, slots)
    gap_flux(found, lambda layer: (fresh[layer, 1, :, LANES - 1 : LANES], fresh[layer, 2, :, 0:1]))
    for copy in edges2[3:]:
        copy.wait_recv()
    fill_edges(edge_layers(edge_in2, corner_in2, 0), edge_layers(edge_in, corner_in, 2), False)
    for copy in layers2:
        copy.wait_recv()
    fill_rows(lambda at, c: (halo2[0, c, at, :], fresh[0, c, at, :], fresh[1, c, at, :], halo2[1, c, at, :]), k_rows, False)

    def put_packed(layer, c, start, new):
        packed[pl.ds(start, CHUNK), layer * 4 + c, :] = new

    sweep(lambda layer, at, c: fresh[layer, c, at, :], put_packed, False)

    hear(3)
    load_order.wait()

    def pick(j):
        send[j] = packed[order_ref[0, j]]

    def target_group(i):
        return jnp.where(i % 2 == 1, groups // 2 - (i + 1) // 2, groups - groups // 2 + i // 2) % groups

    def spread(i, carry):
        other = (mine + target_group(i)) % groups
        for step in range(group):
            pick(other * group + step)
        for step in range(group):
            j = other * group + (place + step) % group
            remote(send.at[j], recv.at[me], spread_send_sem, spread_sem.at[mine], j, y).start()
        return carry

    lax.fori_loop(0, groups - 1, spread, 0)
    for step in range(group):
        pick(mine * group + step)
    for step in range(1, group):
        j = mine * group + (place + step) % group
        remote(send.at[j], recv.at[me], spread_send_sem, spread_sem.at[mine], j, y).start()
    pltpu.make_async_copy(send.at[me], recv.at[me], spread_sem.at[mine]).start()

    load_trial.wait()
    load_active.wait()
    active = jnp.broadcast_to(active_ref[...], (8, LANES))
    upper = lax.broadcasted_iota(jnp.int32, (8, LANES), 0) < 4

    def creep(i, carry):
        g = (mine + groups - target_group(i)) % groups
        at = pl.ds(g * group, group)
        pltpu.make_async_copy(recv.at[at], recv.at[at], spread_sem.at[g]).wait()
        temp = recv[at]
        trial = trial_v[at]
        rate = CREEP_RATE * jnp.exp(-ACTIVATION / (temp + REFERENCE_TEMP))
        slip = jnp.zeros_like(trial)
        for newton in range(NEWTON):
            left = trial - slip
            pull = rate * (left * left)
            slip = slip - (slip - pull * left) / (1.0 + 3.0 * pull)
        sums = []
        for e in range(2):
            live = jnp.where(jnp.full((8, LANES), 2 * g + e, jnp.int32) < active, 1.0, 0.0)
            part = live * slip[4 * e : 4 * e + 4]
            stress_ref[pl.ds(g * group + 4 * e, 4)] = trial[4 * e : 4 * e + 4] - part
            total = part[0] + part[1] + part[2] + part[3]
            sums.append((total + pltpu.roll(total, 4, 0)) * 0.125)
        strain_ref[g] = jnp.where(upper, sums[0], sums[1])
        return carry

    lax.fori_loop(0, groups, creep, 0)
    for copy in edges + layers + edges2 + layers2:
        copy.wait_send()
    most = pl.ds(0, n - 1)
    pltpu.make_async_copy(send.at[most], send.at[most], spread_send_sem).wait()


def hand_over(stress_ref, strain_ref, stress_out, strain_out, sem):
    copies = [
        pltpu.make_async_copy(stress_ref, stress_out, sem.at[0]),
        pltpu.make_async_copy(strain_ref, strain_out, sem.at[1]),
    ]
    for copy in copies:
        copy.start()
    for copy in copies:
        copy.wait()


def solution(mesh):
    slabs, sections, mechs = (mesh.shape[a] for a in ("slab", "iface", "mech"))
    n = slabs * mechs
    groups = n // (2 * mechs)

    def on_device(temp, cond, gap, partner, order, active, trial):
        depth, _, rows, radial = temp.shape
        f32 = jnp.float32
        any_space = pl.BlockSpec(memory_space=pl.ANY)
        hbm = pl.BlockSpec(memory_space=pltpu.HBM)
        vmem = pl.BlockSpec(memory_space=pltpu.VMEM)
        dma = pltpu.SemaphoreType.DMA
        stress, strain = pl.pallas_call(
            functools.partial(kernel, slabs, sections, mechs),
            out_shape=(
                jax.ShapeDtypeStruct((n, 8, LANES), f32),
                jax.ShapeDtypeStruct((groups, 8, LANES), f32),
            ),
            in_specs=[hbm] * 7,
            out_specs=(vmem, vmem),
            scratch_shapes=[
                pltpu.VMEM((depth, rows), f32),
                pltpu.VMEM((1, rows), jnp.int32),
                pltpu.SMEM((1, rows), jnp.int32),
                pltpu.VMEM((1, 1), jnp.int32),
                pltpu.VMEM((2, rows, radial), f32),
                pltpu.VMEM((2, rows, radial), f32),
                pltpu.VMEM((2, 2, rows, radial), f32),
                pltpu.VMEM((2, 4, rows, LANES), f32),
                pltpu.VMEM((2, 4, rows, LANES), f32),
                pltpu.VMEM((2, 3, 4, rows + 2 * PAD, LANES), f32),
                pltpu.VMEM((2, 4, rows, LANES), f32),
                pltpu.VMEM((2, 2, rows, LANES), f32),
                pltpu.VMEM((rows, LANES), f32),
                pltpu.VMEM((8, radial), f32),
                pltpu.VMEM((2 * rows, sections * rows), jnp.bfloat16),
                pltpu.VMEM((2, 8, radial), f32),
                pltpu.VMEM((3, 8, radial), f32),
                pltpu.VMEM((2, 2, 8, radial), f32),
                pltpu.VMEM((2, 8, radial), f32),
                pltpu.VMEM((3, 8, radial), f32),
                pltpu.VMEM((2, 2, 8, radial), f32),
                pltpu.VMEM((rows, 8, LANES), f32),
                pltpu.VMEM((n, 8, LANES), f32),
                pltpu.VMEM((n, 8, LANES), f32),
                pltpu.VMEM((n, 8, LANES), f32),
                dma((7,)),
                dma((20,)),
                dma((2, 2)),
                dma((3,)),
                dma((4,)),
                dma((2,)),
                dma((3,)),
                dma((4,)),
                dma,
                dma((groups,)),
                pltpu.SemaphoreType.REGULAR((4,)),
            ],
            compiler_params=pltpu.CompilerParams(
                collective_id=0, has_side_effects=True, vmem_limit_bytes=48 * 1024 * 1024
            ),
        )(
            *[
                x if x is active else pltpu.with_memory_space_constraint(x, pltpu.HBM)
                for x in (
                    temp.reshape(depth, rows, radial),
                    cond.reshape(depth, rows, radial),
                    gap.reshape(depth, rows),
                    partner.reshape(1, rows),
                    order,
                    active,
                    trial.reshape(n, 8, LANES),
                )
            ]
        )
        stress, strain = pl.pallas_call(
            hand_over,
            out_shape=(
                jax.ShapeDtypeStruct((n, 8, LANES), f32),
                jax.ShapeDtypeStruct((groups, 8, LANES), f32),
            ),
            in_specs=[vmem, vmem],
            out_specs=(any_space, any_space),
            scratch_shapes=[dma((2,))],
            compiler_params=pltpu.CompilerParams(vmem_limit_bytes=8 * 1024 * 1024),
        )(stress, strain)
        return stress.reshape(trial.shape), strain.reshape(trial.shape[0] // 8, 1, 1, radial)

    placed = (
        P(("slab", "mech"), "iface", None, None),
        P(("slab", "mech"), "iface", None, None),
        P(("slab", "mech"), "iface", None),
        P("iface"),
        P("iface", None),
        P("iface", ("slab", "mech")),
        P(None, "iface", ("slab", "mech"), None),
    )
    return jax.shard_map(
        on_device,
        mesh=mesh,
        in_specs=placed,
        out_specs=(
            P(None, "iface", ("slab", "mech"), None),
            P(None, "iface", ("slab", "mech"), None),
        ),
        check_vma=False,
    )
```

```python
import functools

import jax
import jax.numpy as jnp
from jax import lax
from jax.experimental import pallas as pl
from jax.experimental.pallas import tpu as pltpu
from jax.sharding import PartitionSpec as P

MESH = pl.DeviceIdType.MESH
NEWTON = 4
STEP = 0.03
CREEP_RATE = 200.0
ACTIVATION = 12.0
REFERENCE_TEMP = 1.0
LANES = 128
PAD = 8
CHUNK = 32
EARLY = 2
FAR = 5


def kernel(
    slabs,
    sections,
    mechs,
    temp_ref,
    cond_ref,
    gap_in,
    partner_in,
    order_in,
    active_in,
    trial_ref,
    stress_ref,
    strain_ref,
    gap_ref,
    partner_ref,
    order_ref,
    active_ref,
    own_t,
    own_k,
    halo,
    fresh,
    halo2,
    u,
    keep,
    addend,
    cols,
    xbuf,
    hot,
    edge_out,
    edge_in,
    corner_in,
    outer_out,
    outer_in,
    outer_corner,
    inner_out,
    inner_in,
    inner_corner,
    packed,
    send,
    recv,
    trial_v,
    load_sem,
    send_sem,
    layer_sem,
    edge_sem,
    corner_sem,
    layer2_sem,
    outer_sem,
    outer_corner_sem,
    inner_sem,
    inner_corner_sem,
    spread_send_sem,
    spread_sem,
    ready_sem,
):
    n = slabs * mechs
    group = 2 * mechs
    groups = n // group
    rows = own_t.shape[1]
    me = lax.axis_index("slab") * mechs + lax.axis_index("mech")
    y = lax.axis_index("iface")
    mine, place = me // group, me % group
    below, above = (me + n - 1) % n, (me + 1) % n
    y_low, y_high, y_far = (y + sections - 1) % sections, (y + 1) % sections, (y + 2) % sections

    def device(k, section):
        return (k // mechs, section, k % mechs)

    load_t = pltpu.make_async_copy(temp_ref, own_t, load_sem.at[0])
    load_k = pltpu.make_async_copy(cond_ref, own_k, load_sem.at[1])
    load_trial = pltpu.make_async_copy(trial_ref, trial_v, load_sem.at[2])
    load_gap = pltpu.make_async_copy(gap_in, gap_ref, load_sem.at[3])
    load_partner = pltpu.make_async_copy(partner_in, partner_ref, load_sem.at[4])
    load_order = pltpu.make_async_copy(order_in, order_ref, load_sem.at[5])
    load_active = pltpu.make_async_copy(active_in, active_ref, load_sem.at[6])
    for copy in (load_partner, load_gap, load_t, load_k, load_order, load_active):
        copy.start()

    barrier = pltpu.get_barrier_semaphore()

    def greet(k, section):
        pl.semaphore_signal(barrier, inc=1, device_id=device(k, section), device_id_type=MESH)

    near = [
        (below, y), (above, y), (me, y_low), (me, y_high), (me, y_far),
        (below, y_low), (below, y_high), (above, y_low), (above, y_high),
    ]
    for k, section in near:
        greet(k, section)
    for step in range(1, group):
        greet(mine * group + (place + step) % group, y)
    for step in (1, groups - 1):
        greet(((mine + step) % groups) * group + place, y)

    load_trial.start()
    row_of = lax.broadcasted_iota(jnp.int32, (rows, LANES), 0)
    lane_of = lax.broadcasted_iota(jnp.int32, (rows, LANES), 1)
    diagonal = row_of == lane_of

    def as_row(column):
        return jnp.sum(jnp.where(diagonal, column, 0.0), axis=0, keepdims=True)

    def as_column(row):
        return jnp.sum(jnp.where(diagonal, row, 0.0), axis=1, keepdims=True)

    base = (y * rows).astype(jnp.float32)
    whole = float(sections * rows)

    def relative(index):
        shifted = index - base
        return jnp.where(shifted < 0.0, shifted + whole, shifted)

    load_partner.wait()
    load_gap.wait()
    partner_row = partner_ref[...].astype(jnp.float32)
    partner_column = as_column(relative(partner_row))
    cols[:, 0:1] = as_column(gap_ref[0:1, :])
    cols[:, 1:2] = as_column(gap_ref[1:2, :])
    for q in range(sections):
        at = lax.broadcasted_iota(jnp.int32, (rows, LANES), 1).astype(jnp.float32) + float(q * rows)
        hot[0:rows, q * LANES : (q + 1) * LANES] = jnp.where(at == partner_column, 1.0, 0.0).astype(jnp.bfloat16)
    load_t.wait()
    load_k.wait()
    zeros_row = jnp.zeros((1, LANES), jnp.float32)
    for e, at in ((0, 0), (1, rows - 1)):
        for layer in range(2):
            edge_out[e, layer : layer + 1, :] = own_t[layer, at : at + 1, :]
            edge_out[e, 2 + layer : 3 + layer, :] = own_k[layer, at : at + 1, :]
    for layer in range(2):
        compact = as_row(own_t[layer, :, 2 * LANES - 1 : 2 * LANES])
        canister = as_row(own_t[layer, :, 2 * LANES : 2 * LANES + 1])
        for e in range(2):
            edge_out[e, 4:5, layer * LANES : (layer + 1) * LANES] = compact
            edge_out[e, 4:5, (2 + layer) * LANES : (3 + layer) * LANES] = canister
            edge_out[e, 5:6, layer * LANES : (layer + 1) * LANES] = gap_ref[layer : layer + 1, :]
    for e in range(2):
        edge_out[e, 5:6, 2 * LANES : 3 * LANES] = partner_row
        edge_out[e, 5:6, 3 * LANES : 4 * LANES] = zeros_row
        edge_out[e, 6:8, :] = jnp.zeros((2, 4 * LANES), jnp.float32)
        outer_out[e] = jnp.zeros((8, 2 * LANES), jnp.float32)
        inner_out[e] = jnp.zeros((8, 2 * LANES), jnp.float32)
    pl.semaphore_wait(barrier, len(near) + group - 1 + 2)

    def tell(level):
        for step in sorted({2**level, groups - 2**level}):
            other = ((mine + step) % groups) * group + place
            pl.semaphore_signal(ready_sem.at[level], inc=1, device_id=device(other, y), device_id_type=MESH)

    def hear(level):
        pl.semaphore_wait(ready_sem.at[level], len({2**level, groups - 2**level}))

    tell(0)

    def remote(source, target, sent, landed, k, section):
        return pltpu.make_async_remote_copy(
            src_ref=source, dst_ref=target, send_sem=sent, recv_sem=landed,
            device_id=device(k, section), device_id_type=MESH,
        )

    def edge_copies(out, into, corners, edge_landed, corner_landed, first, faces=True):
        across = [remote(out.at[0], into.at[2], send_sem.at[first + 2], edge_landed.at[2], me, y_far)] if faces else []
        return [
            remote(out.at[1], into.at[0], send_sem.at[first], edge_landed.at[0], me, y_high),
            remote(out.at[0], into.at[1], send_sem.at[first + 1], edge_landed.at[1], me, y_low),
            *across,
            remote(out.at[1], corners.at[0, 0], send_sem.at[first + 3], corner_landed.at[0], above, y_high),
            remote(out.at[0], corners.at[0, 1], send_sem.at[first + 4], corner_landed.at[1], above, y_low),
            remote(out.at[1], corners.at[1, 0], send_sem.at[first + 5], corner_landed.at[2], below, y_high),
            remote(out.at[0], corners.at[1, 1], send_sem.at[first + 6], corner_landed.at[3], below, y_low),
        ]

    edges = edge_copies(edge_out, edge_in, corner_in, edge_sem, corner_sem, 0)
    for copy in edges:
        copy.start()

    def half_of(half):
        return pl.ds(2 * half * LANES, 2 * LANES)

    def layer_copies(half):
        out = []
        for f, ref in enumerate((temp_ref, cond_ref)):
            for side, (layer, k) in enumerate(((1, above), (0, below))):
                out.append(
                    remote(
                        ref.at[layer, :, half_of(half)], halo.at[side, f, :, half_of(half)],
                        send_sem.at[7 + 4 * half + 2 * f + side], layer_sem.at[side, f, half], k, y,
                    )
                )
        return out

    layers = [layer_copies(0), layer_copies(1)]
    for copy in layers[0]:
        copy.start()

    has_below = jnp.where(me > 0, 0.5, 0.0).astype(jnp.float32)
    has_above = jnp.where(me < n - 1, 0.5, 0.0).astype(jnp.float32)
    has_low = jnp.where(y > 0, 1.0, 0.0).astype(jnp.float32)
    has_high = jnp.where(y < sections - 1, 1.0, 0.0).astype(jnp.float32)

    def across_layers(before, first, second, after):
        return (
            first + 0.5 * second + has_below * before,
            second + 0.5 * first + has_above * after,
        )

    def fill_edges(t_of, k_of, with_cond, half):
        for e, row, there in ((0, PAD - 1, has_low), (1, PAD + rows, has_high)):
            ts, ks = t_of(e), k_of(e)
            sums = [across_layers(*ts), across_layers(*[a * b for a, b in zip(ts, ks)])]
            if with_cond:
                sums.append(across_layers(*ks))
            for f, pair in enumerate(sums):
                for layer in range(2):
                    edge = there * pair[layer]
                    for j in range(2):
                        u[layer, f, 2 * half + j, row : row + 1, :] = edge[:, j * LANES : (j + 1) * LANES]

    def fill_rows(t_of, k_of, with_cond, half):
        def body(i, carry):
            start = pl.multiple_of(i * CHUNK, CHUNK)
            at = pl.ds(start, CHUNK)
            to = pl.ds(pl.multiple_of(start + PAD, 8), CHUNK)
            for c in (2 * half, 2 * half + 1):
                ts, ks = t_of(at, c), k_of(at, c)
                sums = [across_layers(*ts), across_layers(*[a * b for a, b in zip(ts, ks)])]
                if with_cond:
                    sums.append(across_layers(*ks))
                for f, pair in enumerate(sums):
                    for layer in range(2):
                        u[layer, f, c, to, :] = pair[layer]
            return carry

        lax.fori_loop(0, rows // CHUNK, body, 0)

    lane = lax.broadcasted_iota(jnp.int32, (CHUNK, LANES), 1)
    first_lane, last_lane = lane == 0, lane == LANES - 1

    def spread_of(layer, f, c0, start):
        v = []
        for c in (c0, c0 + 1):
            mid = u[layer, f, c, pl.ds(start + PAD, CHUNK), :]
            up = u[layer, f, c, pl.ds(start + PAD - 1, CHUNK), :]
            down = u[layer, f, c, pl.ds(start + PAD + 1, CHUNK), :]
            v.append(mid + 0.5 * (up + down))
        right = [pltpu.roll(x, 1, 1) for x in v]
        left = [pltpu.roll(x, LANES - 1, 1) for x in v]
        return [
            v[0] + 0.5 * (jnp.where(first_lane, 0.0, right[0]) + jnp.where(last_lane, left[1], left[0])),
            v[1] + 0.5 * (jnp.where(first_lane, right[0], right[1]) + jnp.where(last_lane, 0.0, left[1])),
        ]

    def sweep(t_of, put, first, half, faces):
        for layer in range(2):
            for i in range(rows // CHUNK):
                start = i * CHUNK
                at = pl.ds(start, CHUNK)
                spread_t = spread_of(layer, 0, 2 * half, start)
                spread_kt = spread_of(layer, 1, 2 * half, start)
                spread_k = spread_of(layer, 2, 2 * half, start) if first else None
                for j in range(2):
                    c = 2 * half + j
                    k = own_k[layer, at, c * LANES : (c + 1) * LANES]
                    t = t_of(layer, at, c)
                    if first:
                        weight = jnp.full((CHUNK, LANES), 8.0, jnp.float32)
                        if c == 1:
                            weight = jnp.where(last_lane, 6.0, weight)
                        if c == 2:
                            weight = jnp.where(first_lane, 6.0, weight)
                        drain = weight * k + spread_k[j]
                        keep[layer, c, at, :] = drain
                    else:
                        drain = keep[layer, c, at, :]
                    new = t + STEP * (k * spread_t[j] + spread_kt[j] - t * drain)
                    if c in faces:
                        new = new + addend[layer, c - 1, at, :]
                    put(layer, c, start, new)

    def gather(rows_of, slots):
        for q, slot in enumerate((None, *slots)):
            for i, row in enumerate(rows_of(slot)):
                xbuf[i : i + 1, q * LANES : (q + 1) * LANES] = row
        x = xbuf[...]
        high = x.astype(jnp.bfloat16)
        rest = x - high.astype(jnp.float32)
        middle = rest.astype(jnp.bfloat16)
        low = (rest - middle.astype(jnp.float32)).astype(jnp.bfloat16)
        return sum(
            lax.dot_general(hot[...], part, (((1,), (1,)), ((), ())), preferred_element_type=jnp.float32)
            for part in (high, middle, low)
        )

    def gap_flux(found, face_of):
        for layer in range(2):
            compact, canister = face_of(layer)
            flux = cols[:, layer : layer + 1] * (found[0:rows, layer : layer + 1] - canister)
            returned = cols[:, 2 + layer : 3 + layer] * (compact - found[rows : 2 * rows, 2 + layer : 3 + layer])
            addend[layer, 0] = jnp.where(lane_of == LANES - 1, -STEP * returned, 0.0)
            addend[layer, 1] = jnp.where(lane_of == 0, STEP * flux, 0.0)

    hear(0)
    tell(1)
    xbuf[6:8, :] = jnp.zeros((2, 4 * LANES), jnp.float32)
    for copy in edges[:3]:
        copy.wait_recv()
    slots = (1, 2, 0)

    def start_rows(slot):
        tile = edge_out[0] if slot is None else edge_in[slot]
        return [tile[4:5, i * LANES : (i + 1) * LANES] for i in range(4)] + [
            tile[5:6, i * LANES : (i + 1) * LANES] for i in range(2)
        ]

    for q, tile in enumerate([edge_out[0], *[edge_in[slot] for slot in slots]]):
        theirs = relative(tile[5:6, 2 * LANES : 3 * LANES])
        hot[rows : 2 * rows, q * LANES : (q + 1) * LANES] = jnp.where(
            row_of.astype(jnp.float32) == theirs, 1.0, 0.0
        ).astype(jnp.bfloat16)
    found = gather(start_rows, slots)
    cols[:, 2:4] = found[rows : 2 * rows, 4:6]
    gap_flux(
        found,
        lambda layer: (own_t[layer, :, 2 * LANES - 1 : 2 * LANES], own_t[layer, :, 2 * LANES : 2 * LANES + 1]),
    )
    for copy in layers[1]:
        copy.start()
    for copy in edges[3:]:
        copy.wait_recv()

    def edge_layers(into, corners, row, columns):
        def of(e):
            return (
                corners[0, e, row + 1 : row + 2, columns],
                into[e, row : row + 1, columns],
                into[e, row + 1 : row + 2, columns],
                corners[1, e, row : row + 1, columns],
            )

        return of

    def half_slice(half):
        return slice(2 * half * LANES, 2 * (half + 1) * LANES)

    def block(c):
        return slice(c * LANES, (c + 1) * LANES)

    def k_rows(at, c):
        return (halo[0, 1, at, block(c)], own_k[0, at, block(c)], own_k[1, at, block(c)], halo[1, 1, at, block(c)])

    def t_rows(at, c):
        return (halo[0, 0, at, block(c)], own_t[0, at, block(c)], own_t[1, at, block(c)], halo[1, 0, at, block(c)])

    def put_fresh(layer, c, start, new):
        fresh[layer, c, pl.ds(start, CHUNK), :] = new

    def first_sweep(half):
        columns = half_slice(half)
        fill_edges(
            edge_layers(edge_in, corner_in, 0, columns), edge_layers(edge_in, corner_in, 2, columns), True, half
        )
        for copy in layers[half]:
            copy.wait_recv()
        fill_rows(t_rows, k_rows, True, half)
        sweep(lambda layer, at, c: own_t[layer, at, block(c)], put_fresh, True, half, (1, 2))

    def fresh_copies(half):
        pair = pl.ds(2 * half, 2)
        return [
            remote(fresh.at[1, pair], halo2.at[0, pair], send_sem.at[15 + 2 * half], layer2_sem.at[0, half], above, y),
            remote(fresh.at[0, pair], halo2.at[1, pair], send_sem.at[16 + 2 * half], layer2_sem.at[1, half], below, y),
        ]

    def fresh_edges(out, half):
        for e, at in ((0, 0), (1, rows - 1)):
            for layer in range(2):
                for j in range(2):
                    out[e, layer : layer + 1, block(j)] = fresh[layer, 2 * half + j, at : at + 1, :]

    hear(1)
    tell(2)
    first_sweep(0)
    layers2 = [fresh_copies(0), fresh_copies(1)]
    for copy in layers2[0]:
        copy.start()
    fresh_edges(outer_out, 0)
    outer = edge_copies(outer_out, outer_in, outer_corner, outer_sem, outer_corner_sem, 19, faces=False)
    for copy in outer:
        copy.start()
    hear(2)
    tell(3)
    first_sweep(1)
    for layer in range(2):
        compact = as_row(fresh[layer, 1, :, LANES - 1 : LANES])
        canister = as_row(fresh[layer, 2, :, 0:1])
        for e in range(2):
            inner_out[e, 4:5, block(layer)] = compact
            inner_out[e, 5:6, block(layer)] = canister
    fresh_edges(inner_out, 1)
    inner = edge_copies(inner_out, inner_in, inner_corner, inner_sem, inner_corner_sem, 26)
    for copy in inner:
        copy.start()
    for copy in layers2[1]:
        copy.start()

    def put_packed(layer, c, start, new):
        packed[pl.ds(start, CHUNK), 2 * c + layer, :] = new

    def second_sweep(half, into, corners, faces):
        fill_edges(
            edge_layers(into, corners, 0, slice(0, 2 * LANES)),
            edge_layers(edge_in, corner_in, 2, half_slice(half)),
            False,
            half,
        )
        for copy in layers2[half]:
            copy.wait_recv()
        fill_rows(
            lambda at, c: (halo2[0, c, at, :], fresh[0, c, at, :], fresh[1, c, at, :], halo2[1, c, at, :]),
            k_rows,
            False,
            half,
        )
        sweep(lambda layer, at, c: fresh[layer, c, at, :], put_packed, False, half, faces)

    for copy in outer:
        copy.wait_recv()
    second_sweep(0, outer_in, outer_corner, ())

    hear(3)
    load_order.wait()

    def target_group(i):
        return jnp.where(i % 2 == 1, groups // 2 - (i + 1) // 2, groups - groups // 2 + i // 2) % groups

    def pick(j, first, count):
        send[j, first : first + count] = packed[order_ref[0, j], first : first + count]

    def post(j, first, count, part):
        span = pl.ds(first, count)
        remote(
            send.at[j, span], recv.at[me, span], spread_send_sem.at[part], spread_sem.at[part, mine], j, y
        ).start()

    def spread(begin, end, first, count, part):
        def body(i, carry):
            other = (mine + target_group(i)) % groups
            for step in range(group):
                pick(other * group + step, first, count)
            for step in range(group):
                post(other * group + (place + step) % group, first, count, part)
            return carry

        lax.fori_loop(begin, end, body, 0)

    spread(0, FAR, 0, EARLY, 0)

    for copy in inner[:3]:
        copy.wait_recv()

    def fresh_rows(slot):
        tile = inner_out[0] if slot is None else inner_in[slot]
        return [tile[row : row + 1, block(layer)] for row in (4, 5) for layer in range(2)]

    found = gather(fresh_rows, slots)
    gap_flux(found, lambda layer: (fresh[layer, 1, :, LANES - 1 : LANES], fresh[layer, 2, :, 0:1]))
    for layer in range(2):
        packed[:, 2 + layer, :] = packed[:, 2 + layer, :] + addend[layer, 0]
    for copy in inner[3:]:
        copy.wait_recv()
    second_sweep(1, inner_in, inner_corner, (2,))
    spread(0, FAR, EARLY, 8 - EARLY, 1)
    spread(FAR, groups - 1, 0, 8, 2)
    for step in range(group):
        pick(mine * group + step, 0, 8)
    for step in range(1, group):
        post(mine * group + (place + step) % group, 0, 8, 2)
    pltpu.make_async_copy(send.at[me], recv.at[me], spread_sem.at[2, mine]).start()

    load_trial.wait()
    load_active.wait()
    active = jnp.broadcast_to(active_ref[...], (8, LANES))
    sublane = lax.broadcasted_iota(jnp.int32, (8, LANES), 0)
    in_order = jnp.where(sublane < 4, 2 * sublane, 2 * sublane - 7)
    upper = lax.broadcasted_iota(jnp.int32, (8, LANES), 0) < 4

    def source(i):
        return (mine + groups - target_group(i)) % groups

    def creep_far(i, carry):
        g = source(i)
        at = pl.ds(g * group, group)
        for part, span in enumerate((pl.ds(0, EARLY), pl.ds(EARLY, 8 - EARLY))):
            pltpu.make_async_copy(recv.at[at, span], recv.at[at, span], spread_sem.at[part, g]).wait()
        return creep(g, carry)

    def creep_near(i, carry):
        g = source(i)
        at = pl.ds(g * group, group)
        pltpu.make_async_copy(recv.at[at], recv.at[at], spread_sem.at[2, g]).wait()
        return creep(g, carry)

    def creep(g, carry):
        at = pl.ds(g * group, group)
        temp = jnp.stack([jnp.take_along_axis(recv[g * group + i], in_order, axis=0) for i in range(group)])
        trial = trial_v[at]
        rate = CREEP_RATE * jnp.exp(-ACTIVATION / (temp + REFERENCE_TEMP))
        slip = jnp.zeros_like(trial)
        for newton in range(NEWTON):
            left = trial - slip
            pull = rate * (left * left)
            slip = slip - (slip - pull * left) / (1.0 + 3.0 * pull)
        sums = []
        for e in range(2):
            live = jnp.where(jnp.full((8, LANES), 2 * g + e, jnp.int32) < active, 1.0, 0.0)
            part = live * slip[4 * e : 4 * e + 4]
            stress_ref[pl.ds(g * group + 4 * e, 4)] = trial[4 * e : 4 * e + 4] - part
            total = part[0] + part[1] + part[2] + part[3]
            sums.append((total + pltpu.roll(total, 4, 0)) * 0.125)
        strain_ref[g] = jnp.where(upper, sums[0], sums[1])
        return carry

    lax.fori_loop(0, FAR, creep_far, 0)
    lax.fori_loop(FAR, groups, creep_near, 0)
    for copy in edges + layers[0] + layers[1] + outer + inner + layers2[0] + layers2[1]:
        copy.wait_send()
    far, near_by = pl.ds(0, FAR * group), pl.ds(0, n - 1 - FAR * group)
    for part, sent in enumerate(
        (send.at[far, pl.ds(0, EARLY)], send.at[far, pl.ds(EARLY, 8 - EARLY)], send.at[near_by])
    ):
        pltpu.make_async_copy(sent, sent, spread_send_sem.at[part]).wait()


def hand_over(stress_ref, strain_ref, stress_out, strain_out, sem):
    copies = [
        pltpu.make_async_copy(stress_ref, stress_out, sem.at[0]),
        pltpu.make_async_copy(strain_ref, strain_out, sem.at[1]),
    ]
    for copy in copies:
        copy.start()
    for copy in copies:
        copy.wait()


def solution(mesh):
    slabs, sections, mechs = (mesh.shape[a] for a in ("slab", "iface", "mech"))
    n = slabs * mechs
    groups = n // (2 * mechs)

    def on_device(temp, cond, gap, partner, order, active, trial):
        depth, _, rows, radial = temp.shape
        f32 = jnp.float32
        any_space = pl.BlockSpec(memory_space=pl.ANY)
        hbm = pl.BlockSpec(memory_space=pltpu.HBM)
        vmem = pl.BlockSpec(memory_space=pltpu.VMEM)
        dma = pltpu.SemaphoreType.DMA
        stress, strain = pl.pallas_call(
            functools.partial(kernel, slabs, sections, mechs),
            out_shape=(
                jax.ShapeDtypeStruct((n, 8, LANES), f32),
                jax.ShapeDtypeStruct((groups, 8, LANES), f32),
            ),
            in_specs=[hbm] * 7,
            out_specs=(vmem, vmem),
            scratch_shapes=[
                pltpu.VMEM((depth, rows), f32),
                pltpu.VMEM((1, rows), jnp.int32),
                pltpu.SMEM((1, rows), jnp.int32),
                pltpu.VMEM((1, 1), jnp.int32),
                pltpu.VMEM((2, rows, radial), f32),
                pltpu.VMEM((2, rows, radial), f32),
                pltpu.VMEM((2, 2, rows, radial), f32),
                pltpu.VMEM((2, 4, rows, LANES), f32),
                pltpu.VMEM((2, 4, rows, LANES), f32),
                pltpu.VMEM((2, 3, 4, rows + 2 * PAD, LANES), f32),
                pltpu.VMEM((2, 4, rows, LANES), f32),
                pltpu.VMEM((2, 2, rows, LANES), f32),
                pltpu.VMEM((rows, LANES), f32),
                pltpu.VMEM((8, radial), f32),
                pltpu.VMEM((2 * rows, sections * rows), jnp.bfloat16),
                pltpu.VMEM((2, 8, radial), f32),
                pltpu.VMEM((3, 8, radial), f32),
                pltpu.VMEM((2, 2, 8, radial), f32),
                pltpu.VMEM((2, 8, radial // 2), f32),
                pltpu.VMEM((3, 8, radial // 2), f32),
                pltpu.VMEM((2, 2, 8, radial // 2), f32),
                pltpu.VMEM((2, 8, radial // 2), f32),
                pltpu.VMEM((3, 8, radial // 2), f32),
                pltpu.VMEM((2, 2, 8, radial // 2), f32),
                pltpu.VMEM((rows, 8, LANES), f32),
                pltpu.VMEM((n, 8, LANES), f32),
                pltpu.VMEM((n, 8, LANES), f32),
                pltpu.VMEM((n, 8, LANES), f32),
                dma((7,)),
                dma((33,)),
                dma((2, 2, 2)),
                dma((3,)),
                dma((4,)),
                dma((2, 2)),
                dma((3,)),
                dma((4,)),
                dma((3,)),
                dma((4,)),
                dma((3,)),
                dma((3, groups)),
                pltpu.SemaphoreType.REGULAR((4,)),
            ],
            compiler_params=pltpu.CompilerParams(
                collective_id=0, has_side_effects=True, vmem_limit_bytes=48 * 1024 * 1024
            ),
        )(
            *[
                x if x is active else pltpu.with_memory_space_constraint(x, pltpu.HBM)
                for x in (
                    temp.reshape(depth, rows, radial),
                    cond.reshape(depth, rows, radial),
                    gap.reshape(depth, rows),
                    partner.reshape(1, rows),
                    order,
                    active,
                    trial.reshape(n, 8, LANES),
                )
            ]
        )
        stress, strain = pl.pallas_call(
            hand_over,
            out_shape=(
                jax.ShapeDtypeStruct((n, 8, LANES), f32),
                jax.ShapeDtypeStruct((groups, 8, LANES), f32),
            ),
            in_specs=[vmem, vmem],
            out_specs=(any_space, any_space),
            scratch_shapes=[dma((2,))],
            compiler_params=pltpu.CompilerParams(vmem_limit_bytes=8 * 1024 * 1024),
        )(stress, strain)
        return stress.reshape(trial.shape), strain.reshape(trial.shape[0] // 8, 1, 1, radial)

    placed = (
        P(("slab", "mech"), "iface", None, None),
        P(("slab", "mech"), "iface", None, None),
        P(("slab", "mech"), "iface", None),
        P("iface"),
        P("iface", None),
        P("iface", ("slab", "mech")),
        P(None, "iface", ("slab", "mech"), None),
    )
    return jax.shard_map(
        on_device,
        mesh=mesh,
        in_specs=placed,
        out_specs=(
            P(None, "iface", ("slab", "mech"), None),
            P(None, "iface", ("slab", "mech"), None),
        ),
        check_vma=False,
    )
```

```python
import functools

import jax
import jax.numpy as jnp
from jax import lax
from jax.experimental import pallas as pl
from jax.experimental.pallas import tpu as pltpu
from jax.sharding import PartitionSpec as P

MESH = pl.DeviceIdType.MESH
NEWTON = 4
STEP = 0.03
CREEP_RATE = 200.0
ACTIVATION = 12.0
REFERENCE_TEMP = 1.0
LANES = 128
PAD = 8
CHUNK = 32
EARLY = 2
FAR = 5


def kernel(
    slabs,
    sections,
    mechs,
    temp_ref,
    cond_ref,
    gap_in,
    partner_in,
    order_in,
    active_in,
    trial_ref,
    stress_ref,
    strain_ref,
    gap_ref,
    partner_ref,
    order_ref,
    active_ref,
    own_t,
    own_k,
    halo,
    fresh,
    halo2,
    u,
    keep,
    addend,
    cols,
    xbuf,
    hot,
    edge_out,
    edge_in,
    corner_in,
    outer_out,
    outer_in,
    outer_corner,
    inner_out,
    inner_in,
    inner_corner,
    packed,
    send,
    recv,
    trial_v,
    load_sem,
    send_sem,
    layer_sem,
    edge_sem,
    corner_sem,
    layer2_sem,
    outer_sem,
    outer_corner_sem,
    inner_sem,
    inner_corner_sem,
    spread_send_sem,
    spread_sem,
    ready_sem,
):
    n = slabs * mechs
    group = 2 * mechs
    groups = n // group
    rows = own_t.shape[1]
    me = lax.axis_index("slab") * mechs + lax.axis_index("mech")
    y = lax.axis_index("iface")
    mine, place = me // group, me % group
    below, above = (me + n - 1) % n, (me + 1) % n
    y_low, y_high, y_far = (y + sections - 1) % sections, (y + 1) % sections, (y + 2) % sections

    def device(k, section):
        return (k // mechs, section, k % mechs)

    load_t = pltpu.make_async_copy(temp_ref, own_t, load_sem.at[0])
    load_k = pltpu.make_async_copy(cond_ref, own_k, load_sem.at[1])
    load_trial = pltpu.make_async_copy(trial_ref, trial_v, load_sem.at[2])
    load_gap = pltpu.make_async_copy(gap_in, gap_ref, load_sem.at[3])
    load_partner = pltpu.make_async_copy(partner_in, partner_ref, load_sem.at[4])
    load_order = pltpu.make_async_copy(order_in, order_ref, load_sem.at[5])
    load_active = pltpu.make_async_copy(active_in, active_ref, load_sem.at[6])
    for copy in (load_partner, load_gap, load_t, load_k, load_order, load_active):
        copy.start()

    barrier = pltpu.get_barrier_semaphore()

    def greet(k, section):
        pl.semaphore_signal(barrier, inc=1, device_id=device(k, section), device_id_type=MESH)

    near = [
        (below, y), (above, y), (me, y_low), (me, y_high), (me, y_far),
        (below, y_low), (below, y_high), (above, y_low), (above, y_high),
    ]
    for k, section in near:
        greet(k, section)
    for step in range(1, group):
        greet(mine * group + (place + step) % group, y)
    for step in (1, groups - 1):
        greet(((mine + step) % groups) * group + place, y)

    load_trial.start()
    row_of = lax.broadcasted_iota(jnp.int32, (rows, LANES), 0)
    lane_of = lax.broadcasted_iota(jnp.int32, (rows, LANES), 1)
    diagonal = row_of == lane_of

    def as_row(column):
        return jnp.sum(jnp.where(diagonal, column, 0.0), axis=0, keepdims=True)

    def as_column(row):
        return jnp.sum(jnp.where(diagonal, row, 0.0), axis=1, keepdims=True)

    base = (y * rows).astype(jnp.float32)
    whole = float(sections * rows)

    def relative(index):
        shifted = index - base
        return jnp.where(shifted < 0.0, shifted + whole, shifted)

    load_partner.wait()
    load_gap.wait()
    partner_row = partner_ref[...].astype(jnp.float32)
    partner_column = as_column(relative(partner_row))
    cols[:, 0:1] = as_column(gap_ref[0:1, :])
    cols[:, 1:2] = as_column(gap_ref[1:2, :])
    for q in range(sections):
        at = lax.broadcasted_iota(jnp.int32, (rows, LANES), 1).astype(jnp.float32) + float(q * rows)
        hot[0:rows, q * LANES : (q + 1) * LANES] = jnp.where(at == partner_column, 1.0, 0.0).astype(jnp.bfloat16)
    load_t.wait()
    load_k.wait()
    zeros_row = jnp.zeros((1, LANES), jnp.float32)
    for e, at in ((0, 0), (1, rows - 1)):
        for layer in range(2):
            edge_out[e, layer : layer + 1, :] = own_t[layer, at : at + 1, :]
            edge_out[e, 2 + layer : 3 + layer, :] = own_k[layer, at : at + 1, :]
    for layer in range(2):
        compact = as_row(own_t[layer, :, 2 * LANES - 1 : 2 * LANES])
        canister = as_row(own_t[layer, :, 2 * LANES : 2 * LANES + 1])
        for e in range(2):
            edge_out[e, 4:5, layer * LANES : (layer + 1) * LANES] = compact
            edge_out[e, 4:5, (2 + layer) * LANES : (3 + layer) * LANES] = canister
            edge_out[e, 5:6, layer * LANES : (layer + 1) * LANES] = gap_ref[layer : layer + 1, :]
    for e in range(2):
        edge_out[e, 5:6, 2 * LANES : 3 * LANES] = partner_row
        edge_out[e, 5:6, 3 * LANES : 4 * LANES] = zeros_row
        edge_out[e, 6:8, :] = jnp.zeros((2, 4 * LANES), jnp.float32)
        outer_out[e] = jnp.zeros((8, 2 * LANES), jnp.float32)
        inner_out[e] = jnp.zeros((8, 2 * LANES), jnp.float32)
    pl.semaphore_wait(barrier, len(near) + group - 1 + 2)

    def tell(level):
        for step in sorted({2**level, groups - 2**level}):
            other = ((mine + step) % groups) * group + place
            pl.semaphore_signal(ready_sem.at[level], inc=1, device_id=device(other, y), device_id_type=MESH)

    def hear(level):
        pl.semaphore_wait(ready_sem.at[level], len({2**level, groups - 2**level}))

    tell(0)

    def remote(source, target, sent, landed, k, section):
        return pltpu.make_async_remote_copy(
            src_ref=source, dst_ref=target, send_sem=sent, recv_sem=landed,
            device_id=device(k, section), device_id_type=MESH,
        )

    def edge_copies(out, into, corners, edge_landed, corner_landed, first, faces=True):
        across = [remote(out.at[0], into.at[2], send_sem.at[first + 2], edge_landed.at[2], me, y_far)] if faces else []
        return [
            remote(out.at[1], into.at[0], send_sem.at[first], edge_landed.at[0], me, y_high),
            remote(out.at[0], into.at[1], send_sem.at[first + 1], edge_landed.at[1], me, y_low),
            *across,
            remote(out.at[1], corners.at[0, 0], send_sem.at[first + 3], corner_landed.at[0], above, y_high),
            remote(out.at[0], corners.at[0, 1], send_sem.at[first + 4], corner_landed.at[1], above, y_low),
            remote(out.at[1], corners.at[1, 0], send_sem.at[first + 5], corner_landed.at[2], below, y_high),
            remote(out.at[0], corners.at[1, 1], send_sem.at[first + 6], corner_landed.at[3], below, y_low),
        ]

    edges = edge_copies(edge_out, edge_in, corner_in, edge_sem, corner_sem, 0)
    for copy in edges:
        copy.start()

    def half_of(half):
        return pl.ds(2 * half * LANES, 2 * LANES)

    def layer_copies(half):
        out = []
        for f, ref in enumerate((temp_ref, cond_ref)):
            for side, (layer, k) in enumerate(((1, above), (0, below))):
                out.append(
                    remote(
                        ref.at[layer, :, half_of(half)], halo.at[side, f, :, half_of(half)],
                        send_sem.at[7 + 4 * half + 2 * f + side], layer_sem.at[side, f, half], k, y,
                    )
                )
        return out

    layers = [layer_copies(0), layer_copies(1)]
    for copy in layers[0] + layers[1]:
        copy.start()

    has_below = jnp.where(me > 0, 0.5, 0.0).astype(jnp.float32)
    has_above = jnp.where(me < n - 1, 0.5, 0.0).astype(jnp.float32)
    has_low = jnp.where(y > 0, 1.0, 0.0).astype(jnp.float32)
    has_high = jnp.where(y < sections - 1, 1.0, 0.0).astype(jnp.float32)

    def across_layers(before, first, second, after):
        return (
            first + 0.5 * second + has_below * before,
            second + 0.5 * first + has_above * after,
        )

    def fill_edges(t_of, k_of, with_cond, half):
        for e, row, there in ((0, PAD - 1, has_low), (1, PAD + rows, has_high)):
            ts, ks = t_of(e), k_of(e)
            sums = [across_layers(*ts), across_layers(*[a * b for a, b in zip(ts, ks)])]
            if with_cond:
                sums.append(across_layers(*ks))
            for f, pair in enumerate(sums):
                for layer in range(2):
                    edge = there * pair[layer]
                    for j in range(2):
                        u[layer, f, 2 * half + j, row : row + 1, :] = edge[:, j * LANES : (j + 1) * LANES]

    def fill_rows(t_of, k_of, with_cond, half):
        def body(i, carry):
            start = pl.multiple_of(i * CHUNK, CHUNK)
            at = pl.ds(start, CHUNK)
            to = pl.ds(pl.multiple_of(start + PAD, 8), CHUNK)
            for c in (2 * half, 2 * half + 1):
                ts, ks = t_of(at, c), k_of(at, c)
                sums = [across_layers(*ts), across_layers(*[a * b for a, b in zip(ts, ks)])]
                if with_cond:
                    sums.append(across_layers(*ks))
                for f, pair in enumerate(sums):
                    for layer in range(2):
                        u[layer, f, c, to, :] = pair[layer]
            return carry

        lax.fori_loop(0, rows // CHUNK, body, 0)

    lane = lax.broadcasted_iota(jnp.int32, (CHUNK, LANES), 1)
    first_lane, last_lane = lane == 0, lane == LANES - 1

    def spread_of(layer, f, c0, start):
        v = []
        for c in (c0, c0 + 1):
            mid = u[layer, f, c, pl.ds(start + PAD, CHUNK), :]
            up = u[layer, f, c, pl.ds(start + PAD - 1, CHUNK), :]
            down = u[layer, f, c, pl.ds(start + PAD + 1, CHUNK), :]
            v.append(mid + 0.5 * (up + down))
        right = [pltpu.roll(x, 1, 1) for x in v]
        left = [pltpu.roll(x, LANES - 1, 1) for x in v]
        return [
            v[0] + 0.5 * (jnp.where(first_lane, 0.0, right[0]) + jnp.where(last_lane, left[1], left[0])),
            v[1] + 0.5 * (jnp.where(first_lane, right[0], right[1]) + jnp.where(last_lane, 0.0, left[1])),
        ]

    def sweep(t_of, put, first, half, faces):
        for layer in range(2):
            for i in range(rows // CHUNK):
                start = i * CHUNK
                at = pl.ds(start, CHUNK)
                spread_t = spread_of(layer, 0, 2 * half, start)
                spread_kt = spread_of(layer, 1, 2 * half, start)
                spread_k = spread_of(layer, 2, 2 * half, start) if first else None
                for j in range(2):
                    c = 2 * half + j
                    k = own_k[layer, at, c * LANES : (c + 1) * LANES]
                    t = t_of(layer, at, c)
                    if first:
                        weight = jnp.full((CHUNK, LANES), 8.0, jnp.float32)
                        if c == 1:
                            weight = jnp.where(last_lane, 6.0, weight)
                        if c == 2:
                            weight = jnp.where(first_lane, 6.0, weight)
                        drain = weight * k + spread_k[j]
                        keep[layer, c, at, :] = drain
                    else:
                        drain = keep[layer, c, at, :]
                    new = t + STEP * (k * spread_t[j] + spread_kt[j] - t * drain)
                    if c in faces:
                        new = new + addend[layer, c - 1, at, :]
                    put(layer, c, start, new)

    def gather(rows_of, slots):
        for q, slot in enumerate((None, *slots)):
            for i, row in enumerate(rows_of(slot)):
                xbuf[i : i + 1, q * LANES : (q + 1) * LANES] = row
        x = xbuf[...]
        high = x.astype(jnp.bfloat16)
        rest = x - high.astype(jnp.float32)
        middle = rest.astype(jnp.bfloat16)
        low = (rest - middle.astype(jnp.float32)).astype(jnp.bfloat16)
        return sum(
            lax.dot_general(hot[...], part, (((1,), (1,)), ((), ())), preferred_element_type=jnp.float32)
            for part in (high, middle, low)
        )

    def gap_flux(found, face_of):
        for layer in range(2):
            compact, canister = face_of(layer)
            flux = cols[:, layer : layer + 1] * (found[0:rows, layer : layer + 1] - canister)
            returned = cols[:, 2 + layer : 3 + layer] * (compact - found[rows : 2 * rows, 2 + layer : 3 + layer])
            addend[layer, 0] = jnp.where(lane_of == LANES - 1, -STEP * returned, 0.0)
            addend[layer, 1] = jnp.where(lane_of == 0, STEP * flux, 0.0)

    hear(0)
    tell(1)
    xbuf[6:8, :] = jnp.zeros((2, 4 * LANES), jnp.float32)
    for copy in edges[:3]:
        copy.wait_recv()
    hear(1)
    tell(2)
    slots = (1, 2, 0)

    def start_rows(slot):
        tile = edge_out[0] if slot is None else edge_in[slot]
        return [tile[4:5, i * LANES : (i + 1) * LANES] for i in range(4)] + [
            tile[5:6, i * LANES : (i + 1) * LANES] for i in range(2)
        ]

    for q, tile in enumerate([edge_out[0], *[edge_in[slot] for slot in slots]]):
        theirs = relative(tile[5:6, 2 * LANES : 3 * LANES])
        hot[rows : 2 * rows, q * LANES : (q + 1) * LANES] = jnp.where(
            row_of.astype(jnp.float32) == theirs, 1.0, 0.0
        ).astype(jnp.bfloat16)
    found = gather(start_rows, slots)
    cols[:, 2:4] = found[rows : 2 * rows, 4:6]
    gap_flux(
        found,
        lambda layer: (own_t[layer, :, 2 * LANES - 1 : 2 * LANES], own_t[layer, :, 2 * LANES : 2 * LANES + 1]),
    )
    hear(2)
    tell(3)
    for copy in edges[3:]:
        copy.wait_recv()

    def edge_layers(into, corners, row, columns):
        def of(e):
            return (
                corners[0, e, row + 1 : row + 2, columns],
                into[e, row : row + 1, columns],
                into[e, row + 1 : row + 2, columns],
                corners[1, e, row : row + 1, columns],
            )

        return of

    def half_slice(half):
        return slice(2 * half * LANES, 2 * (half + 1) * LANES)

    def block(c):
        return slice(c * LANES, (c + 1) * LANES)

    def k_rows(at, c):
        return (halo[0, 1, at, block(c)], own_k[0, at, block(c)], own_k[1, at, block(c)], halo[1, 1, at, block(c)])

    def t_rows(at, c):
        return (halo[0, 0, at, block(c)], own_t[0, at, block(c)], own_t[1, at, block(c)], halo[1, 0, at, block(c)])

    def put_fresh(layer, c, start, new):
        fresh[layer, c, pl.ds(start, CHUNK), :] = new

    def first_sweep(half):
        columns = half_slice(half)
        fill_edges(
            edge_layers(edge_in, corner_in, 0, columns), edge_layers(edge_in, corner_in, 2, columns), True, half
        )
        for copy in layers[half]:
            copy.wait_recv()
        fill_rows(t_rows, k_rows, True, half)
        sweep(lambda layer, at, c: own_t[layer, at, block(c)], put_fresh, True, half, (1, 2))

    def fresh_copies(half):
        pair = pl.ds(2 * half, 2)
        return [
            remote(fresh.at[1, pair], halo2.at[0, pair], send_sem.at[15 + 2 * half], layer2_sem.at[0, half], above, y),
            remote(fresh.at[0, pair], halo2.at[1, pair], send_sem.at[16 + 2 * half], layer2_sem.at[1, half], below, y),
        ]

    def fresh_edges(out, half):
        for e, at in ((0, 0), (1, rows - 1)):
            for layer in range(2):
                for j in range(2):
                    out[e, layer : layer + 1, block(j)] = fresh[layer, 2 * half + j, at : at + 1, :]

    first_sweep(0)
    layers2 = [fresh_copies(0), fresh_copies(1)]
    for copy in layers2[0]:
        copy.start()
    fresh_edges(outer_out, 0)
    outer = edge_copies(outer_out, outer_in, outer_corner, outer_sem, outer_corner_sem, 19, faces=False)
    for copy in outer:
        copy.start()
    first_sweep(1)
    for layer in range(2):
        compact = as_row(fresh[layer, 1, :, LANES - 1 : LANES])
        canister = as_row(fresh[layer, 2, :, 0:1])
        for e in range(2):
            inner_out[e, 4:5, block(layer)] = compact
            inner_out[e, 5:6, block(layer)] = canister
    fresh_edges(inner_out, 1)
    inner = edge_copies(inner_out, inner_in, inner_corner, inner_sem, inner_corner_sem, 26)
    for copy in inner:
        copy.start()
    for copy in layers2[1]:
        copy.start()

    def put_packed(layer, c, start, new):
        packed[pl.ds(start, CHUNK), 2 * c + layer, :] = new

    def second_sweep(half, into, corners, faces):
        fill_edges(
            edge_layers(into, corners, 0, slice(0, 2 * LANES)),
            edge_layers(edge_in, corner_in, 2, half_slice(half)),
            False,
            half,
        )
        for copy in layers2[half]:
            copy.wait_recv()
        fill_rows(
            lambda at, c: (halo2[0, c, at, :], fresh[0, c, at, :], fresh[1, c, at, :], halo2[1, c, at, :]),
            k_rows,
            False,
            half,
        )
        sweep(lambda layer, at, c: fresh[layer, c, at, :], put_packed, False, half, faces)

    for copy in outer:
        copy.wait_recv()
    second_sweep(0, outer_in, outer_corner, ())

    load_order.wait()

    def target_group(i):
        i = jnp.where(i < FAR - 1, i + 1, jnp.where(i == FAR - 1, 0, i))
        return jnp.where(i % 2 == 1, groups // 2 - (i + 1) // 2, groups - groups // 2 + i // 2) % groups

    def pick(j, first, count):
        send[j, first : first + count] = packed[order_ref[0, j], first : first + count]

    def post(j, first, count, part):
        span = pl.ds(first, count)
        remote(
            send.at[j, span], recv.at[me, span], spread_send_sem.at[part], spread_sem.at[part, mine], j, y
        ).start()

    def spread(begin, end, first, count, part):
        def body(i, carry):
            other = (mine + target_group(i)) % groups
            for step in range(group):
                pick(other * group + step, first, count)
            for step in range(group):
                post(other * group + (place + step) % group, first, count, part)
            return carry

        lax.fori_loop(begin, end, body, 0)

    spread(0, FAR - 1, 0, EARLY, 0)
    hear(3)
    spread(FAR - 1, FAR, 0, EARLY, 0)

    for copy in inner[:3]:
        copy.wait_recv()

    def fresh_rows(slot):
        tile = inner_out[0] if slot is None else inner_in[slot]
        return [tile[row : row + 1, block(layer)] for row in (4, 5) for layer in range(2)]

    found = gather(fresh_rows, slots)
    gap_flux(found, lambda layer: (fresh[layer, 1, :, LANES - 1 : LANES], fresh[layer, 2, :, 0:1]))
    for layer in range(2):
        packed[:, 2 + layer, :] = packed[:, 2 + layer, :] + addend[layer, 0]
    for copy in inner[3:]:
        copy.wait_recv()
    second_sweep(1, inner_in, inner_corner, (2,))
    spread(0, FAR, EARLY, 8 - EARLY, 1)
    spread(FAR, groups - 1, 0, 8, 2)
    for step in range(group):
        pick(mine * group + step, 0, 8)
    for step in range(1, group):
        post(mine * group + (place + step) % group, 0, 8, 2)
    pltpu.make_async_copy(send.at[me], recv.at[me], spread_sem.at[2, mine]).start()

    load_trial.wait()
    load_active.wait()
    active = jnp.broadcast_to(active_ref[...], (8, LANES))
    sublane = lax.broadcasted_iota(jnp.int32, (8, LANES), 0)
    in_order = jnp.where(sublane < 4, 2 * sublane, 2 * sublane - 7)
    upper = lax.broadcasted_iota(jnp.int32, (8, LANES), 0) < 4

    def source(i):
        return (mine + groups - target_group(i)) % groups

    def creep_far(i, carry):
        g = source(i)
        at = pl.ds(g * group, group)
        for part, span in enumerate((pl.ds(0, EARLY), pl.ds(EARLY, 8 - EARLY))):
            pltpu.make_async_copy(recv.at[at, span], recv.at[at, span], spread_sem.at[part, g]).wait()
        return creep(g, carry)

    def creep_near(i, carry):
        g = source(i)
        at = pl.ds(g * group, group)
        pltpu.make_async_copy(recv.at[at], recv.at[at], spread_sem.at[2, g]).wait()
        return creep(g, carry)

    def creep(g, carry):
        at = pl.ds(g * group, group)
        temp = jnp.stack([jnp.take_along_axis(recv[g * group + i], in_order, axis=0) for i in range(group)])
        trial = trial_v[at]
        rate = CREEP_RATE * jnp.exp(-ACTIVATION / (temp + REFERENCE_TEMP))
        slip = jnp.zeros_like(trial)
        for newton in range(NEWTON):
            left = trial - slip
            pull = rate * (left * left)
            slip = slip - (slip - pull * left) / (1.0 + 3.0 * pull)
        sums = []
        for e in range(2):
            live = jnp.where(jnp.full((8, LANES), 2 * g + e, jnp.int32) < active, 1.0, 0.0)
            part = live * slip[4 * e : 4 * e + 4]
            stress_ref[pl.ds(g * group + 4 * e, 4)] = trial[4 * e : 4 * e + 4] - part
            total = part[0] + part[1] + part[2] + part[3]
            sums.append((total + pltpu.roll(total, 4, 0)) * 0.125)
        strain_ref[g] = jnp.where(upper, sums[0], sums[1])
        return carry

    lax.fori_loop(0, FAR, creep_far, 0)
    lax.fori_loop(FAR, groups, creep_near, 0)
    for copy in edges + layers[0] + layers[1] + outer + inner + layers2[0] + layers2[1]:
        copy.wait_send()
    far, near_by = pl.ds(0, FAR * group), pl.ds(0, n - 1 - FAR * group)
    for part, sent in enumerate(
        (send.at[far, pl.ds(0, EARLY)], send.at[far, pl.ds(EARLY, 8 - EARLY)], send.at[near_by])
    ):
        pltpu.make_async_copy(sent, sent, spread_send_sem.at[part]).wait()


def hand_over(stress_ref, strain_ref, stress_out, strain_out, sem):
    copies = [
        pltpu.make_async_copy(stress_ref, stress_out, sem.at[0]),
        pltpu.make_async_copy(strain_ref, strain_out, sem.at[1]),
    ]
    for copy in copies:
        copy.start()
    for copy in copies:
        copy.wait()


def solution(mesh):
    slabs, sections, mechs = (mesh.shape[a] for a in ("slab", "iface", "mech"))
    n = slabs * mechs
    groups = n // (2 * mechs)

    def on_device(temp, cond, gap, partner, order, active, trial):
        depth, _, rows, radial = temp.shape
        f32 = jnp.float32
        any_space = pl.BlockSpec(memory_space=pl.ANY)
        hbm = pl.BlockSpec(memory_space=pltpu.HBM)
        vmem = pl.BlockSpec(memory_space=pltpu.VMEM)
        dma = pltpu.SemaphoreType.DMA
        stress, strain = pl.pallas_call(
            functools.partial(kernel, slabs, sections, mechs),
            out_shape=(
                jax.ShapeDtypeStruct((n, 8, LANES), f32),
                jax.ShapeDtypeStruct((groups, 8, LANES), f32),
            ),
            in_specs=[hbm] * 7,
            out_specs=(vmem, vmem),
            scratch_shapes=[
                pltpu.VMEM((depth, rows), f32),
                pltpu.VMEM((1, rows), jnp.int32),
                pltpu.SMEM((1, rows), jnp.int32),
                pltpu.VMEM((1, 1), jnp.int32),
                pltpu.VMEM((2, rows, radial), f32),
                pltpu.VMEM((2, rows, radial), f32),
                pltpu.VMEM((2, 2, rows, radial), f32),
                pltpu.VMEM((2, 4, rows, LANES), f32),
                pltpu.VMEM((2, 4, rows, LANES), f32),
                pltpu.VMEM((2, 3, 4, rows + 2 * PAD, LANES), f32),
                pltpu.VMEM((2, 4, rows, LANES), f32),
                pltpu.VMEM((2, 2, rows, LANES), f32),
                pltpu.VMEM((rows, LANES), f32),
                pltpu.VMEM((8, radial), f32),
                pltpu.VMEM((2 * rows, sections * rows), jnp.bfloat16),
                pltpu.VMEM((2, 8, radial), f32),
                pltpu.VMEM((3, 8, radial), f32),
                pltpu.VMEM((2, 2, 8, radial), f32),
                pltpu.VMEM((2, 8, radial // 2), f32),
                pltpu.VMEM((3, 8, radial // 2), f32),
                pltpu.VMEM((2, 2, 8, radial // 2), f32),
                pltpu.VMEM((2, 8, radial // 2), f32),
                pltpu.VMEM((3, 8, radial // 2), f32),
                pltpu.VMEM((2, 2, 8, radial // 2), f32),
                pltpu.VMEM((rows, 8, LANES), f32),
                pltpu.VMEM((n, 8, LANES), f32),
                pltpu.VMEM((n, 8, LANES), f32),
                pltpu.VMEM((n, 8, LANES), f32),
                dma((7,)),
                dma((33,)),
                dma((2, 2, 2)),
                dma((3,)),
                dma((4,)),
                dma((2, 2)),
                dma((3,)),
                dma((4,)),
                dma((3,)),
                dma((4,)),
                dma((3,)),
                dma((3, groups)),
                pltpu.SemaphoreType.REGULAR((4,)),
            ],
            compiler_params=pltpu.CompilerParams(
                collective_id=0, has_side_effects=True, vmem_limit_bytes=48 * 1024 * 1024
            ),
        )(
            *[
                x if x is active else pltpu.with_memory_space_constraint(x, pltpu.HBM)
                for x in (
                    temp.reshape(depth, rows, radial),
                    cond.reshape(depth, rows, radial),
                    gap.reshape(depth, rows),
                    partner.reshape(1, rows),
                    order,
                    active,
                    trial.reshape(n, 8, LANES),
                )
            ]
        )
        stress, strain = pl.pallas_call(
            hand_over,
            out_shape=(
                jax.ShapeDtypeStruct((n, 8, LANES), f32),
                jax.ShapeDtypeStruct((groups, 8, LANES), f32),
            ),
            in_specs=[vmem, vmem],
            out_specs=(any_space, any_space),
            scratch_shapes=[dma((2,))],
            compiler_params=pltpu.CompilerParams(vmem_limit_bytes=8 * 1024 * 1024),
        )(stress, strain)
        return stress.reshape(trial.shape), strain.reshape(trial.shape[0] // 8, 1, 1, radial)

    placed = (
        P(("slab", "mech"), "iface", None, None),
        P(("slab", "mech"), "iface", None, None),
        P(("slab", "mech"), "iface", None),
        P("iface"),
        P("iface", None),
        P("iface", ("slab", "mech")),
        P(None, "iface", ("slab", "mech"), None),
    )
    return jax.shard_map(
        on_device,
        mesh=mesh,
        in_specs=placed,
        out_specs=(
            P(None, "iface", ("slab", "mech"), None),
            P(None, "iface", ("slab", "mech"), None),
        ),
        check_vma=False,
    )
```
